32 devices in a mesh: groups: 2 (over y), row: 4 (over z), col: 2 (over x), sub: 2 (over core).
Axes of the slice: x: 2, y: 2, z: 4, core: 2. Of those that a mesh axis runs over, the one named last changes fastest.
Arguments:
- orbital_factors: bfloat16 [2, 22528, 2048], P('sub', ('groups', 'col', 'row')), parts along dimension 1, may hold values from -0.8984375 to 0.8984375
- screen_mask: int32 [176, 2], P('groups'), parts along dimension 0, may hold values 0 or 1
Outputs:
- exchange_tiles: float32 [2, 11264, 11264], P(None, ('groups', 'row'), ('col', 'sub')), parts along dimension 1
The draws below stay inside these ranges and needn't reach their ends.
There are 2 independent parts, one for each index of `groups`. The reference program is written for one: setup_inputs(seed, part) draws one part's arguments, and reference() takes and returns one part's arrays. A program takes and returns all parts, laid end to end along the dimension named above; each array names one. Nothing has to cross between parts.
All inputs are finite; a program needn't handle non-finite values.
Results may differ from the reference program's by a relative error of at most 0.0003.
Values may be sent and summed in bfloat16 or wider, within the bound.
No kernel may reach another device: no remote copies, remote signals or barrier semaphores. Data moves between devices by JAX's collectives and lax.ppermute only.
A program may use at most 256 MiB of HBM per device.

```python
import jax
import jax.numpy as jnp

N = 11264
OCC = 2048
AUX = 2
BLK = 128
N_COL = 2


def set_ends(values, stream_key, smallest, largest):
    extent = values.shape
    spot = [jax.random.randint(jax.random.fold_in(stream_key, axis), (), 0, extent[axis]) for axis in range(len(extent))]
    values = values.at[tuple(spot)].set(smallest)
    longest = extent.index(max(extent))
    spot[longest] = (spot[longest] + 1) % extent[longest]
    return values.at[tuple(spot)].set(largest)


def steps_of(key, shape, pieces, smallest, largest):
    gain = 1.0
    for position, shards_of in pieces:
        heights = jax.random.uniform(jax.random.fold_in(jax.random.fold_in(key, 6), position), (shards_of,), jnp.float32, smallest / len(pieces), largest / len(pieces))
        gain = gain * jnp.repeat(jnp.exp(heights), shape[position] // shards_of).reshape((-1,) + (1,) * (len(shape) - 1 - position))
    return gain


def scatter_about(key, shape, width, reach, pieces=(), kind=jnp.bfloat16):
    values = jax.random.normal(key, shape, jnp.float32) * width
    if len(pieces) > 0:
        values = steps_of(key, shape, pieces, -0.22, 0.18) * values
    return jnp.clip(values, min=-reach, max=reach).astype(kind)


def setup_inputs(seed: int = 0, part: int = 0) -> dict:
    splits = jax.random.split(jax.random.key(seed), 3)
    part_keys = jax.random.split(jax.random.fold_in(splits[2], part), 3)
    orbital_factors = scatter_about(part_keys[0], (AUX, N, OCC), 0.15, 0.8984375, ((0, 2), (1, 8)))
    screen_mask = set_ends((jax.random.randint(part_keys[1], (N // BLK, AUX), 0, 4) < 3).astype(jnp.int32), jax.random.fold_in(part_keys[1], 1), 0, 1)
    return {"orbital_factors": orbital_factors, "screen_mask": screen_mask}


def reference(orbital_factors, screen_mask):
    total_rows = orbital_factors.shape[1]
    block_ids = jnp.arange(total_rows, dtype=jnp.int32) // BLK
    row_weights = screen_mask[block_ids].astype(jnp.float32)
    screened = (orbital_factors.astype(jnp.float32) * jnp.transpose(row_weights)[:, :, None]).astype(jnp.bfloat16)
    matrix = jnp.transpose(screened, (1, 0, 2)).reshape(total_rows, -1)
    exchange = jnp.dot(matrix, jnp.transpose(matrix), preferred_element_type=jnp.float32)
    return exchange.reshape(N_COL, total_rows // N_COL, total_rows)
```

```python
import functools

import jax
import jax.numpy as jnp
from jax import lax
from jax.experimental import pallas as pl
from jax.experimental.pallas import tpu as pltpu
from jax.sharding import PartitionSpec as P

BLK = 128
AXES = ("row", "col", "sub")
TILES = 4
GROUPS = 4
EXPS = 16
VMEM_LIMIT = 63 * 2**20


def apply_screen(panel, first_row, screen_mask, aux_start):
    row_total = panel.shape[1]
    block_ids = (first_row + jnp.arange(row_total, dtype=jnp.int32)) // BLK
    one_hot = (
        block_ids[:, None] == jnp.arange(screen_mask.shape[0], dtype=jnp.int32)[None, :]
    ).astype(jnp.float32)
    row_weights = jnp.dot(
        one_hot, screen_mask.astype(jnp.float32), preferred_element_type=jnp.float32
    )
    row_weights = lax.dynamic_slice_in_dim(row_weights, aux_start, panel.shape[0], 1)
    return panel * jnp.transpose(row_weights).astype(jnp.bfloat16)[:, :, None]


def gathered_shards(orbital_factors, screen_mask):
    aux_half, own_rows, occupied = orbital_factors.shape
    row_count = lax.axis_size("row")
    col_count = lax.axis_size("col")
    row_pos = lax.axis_index("row")
    col_pos = lax.axis_index("col")
    sub_pos = lax.axis_index("sub")
    own_first = (col_pos * row_count + row_pos) * own_rows
    screened = apply_screen(orbital_factors, own_first, screen_mask, sub_pos * aux_half)
    contract_dims = (((0, 2), (0, 2)), ((), ()))
    gathered_rows = lax.all_gather(screened, "col", axis=1, tiled=True)
    partial_tile = lax.dot_general(
        gathered_rows,
        lax.all_gather(screened, "row", axis=1, tiled=True),
        contract_dims,
        preferred_element_type=jnp.float32,
    )
    tile_sum = lax.psum_scatter(partial_tile, "sub", scatter_dimension=1, tiled=True)
    return tile_sum.reshape(col_count, own_rows, tile_sum.shape[1])


RESULT, CODED, ARRIVE, FAR, BASE1, BASE2, COLUMN = range(7)


def encode(acc, group):
    coded, exps = [], []
    for g in range(GROUPS):
        part = acc[g * group : (g + 1) * group]
        top = jnp.max(jnp.abs(part), axis=0, keepdims=True)
        exp = jnp.floor(jnp.log2(jnp.maximum(top, 2.0**-100))) + 1.0
        scaled = jnp.round(part * jnp.exp2(15.0 - exp))
        coded.append(jnp.clip(scaled, -32767.0, 32767.0).astype(jnp.int32))
        exps.append(exp)
    return jnp.concatenate(coded, axis=0).astype(jnp.int16), exps


def overlap(segments, lo, hi):
    parts = []
    for k, (off, size) in enumerate(segments):
        first, last = max(lo, off), min(hi, off + size)
        if first < last:
            parts.append((k, first - off, last - first, first - lo))
    return parts


def mm_kernel(send, chunks, blocks, second, which, row_layout, col_layout, *refs):
    it = iter(refs)
    flags = next(it)
    next(it)
    rows = [[[next(it) for _ in range(2)] for _ in segments] for segments in row_layout]
    cols = [[[next(it) for _ in range(2)] for _ in sources] for sources in col_layout]
    rest = list(it)
    if send:
        out, token, rowbuf, colbuf, obuf, ebuf, ecode, rsem, csem, osem, esem = rest
    else:
        out, token, rowbuf, colbuf, obuf, rsem, csem, osem = rest[-8:]
    pieces = [chunks[k] for k in which]
    block_rows = sum(n for _, n in chunks)
    depth = rows[0][0][0].shape[1]
    tile = block_rows // TILES
    width = sum(n for _, n in pieces)
    first_col = pieces[0][0]
    steps = TILES // 2 if send else TILES
    token[...] = jnp.zeros_like(token)

    def col_copy(p, aux, core):
        local = pieces[p][0] - first_col
        return pltpu.make_async_copy(
            cols[p][core][aux].at[pl.ds(col_layout[p][core][aux], pieces[p][1]), :],
            colbuf.at[pl.ds(local, pieces[p][1]), pl.ds(aux * depth, depth)],
            csem.at[p, aux],
        )

    def row_copies(b, i, core):
        lo = (core * steps + i) * tile
        made = []
        spans = [(off, size) for off, size, _ in row_layout[b]]
        for j, (k, off, size, local) in enumerate(overlap(spans, lo, lo + tile)):
            for aux in range(2):
                made.append(
                    pltpu.make_async_copy(
                        rows[b][k][aux].at[pl.ds(row_layout[b][k][2][aux] + off, size), :],
                        rowbuf.at[b, pl.ds(i * tile + local, size), pl.ds(aux * depth, depth)],
                        rsem.at[b, i, j, aux],
                    )
                )
        return made

    def per_core(act):
        for core in range(2):

            @pl.when(flags[FAR] == core)
            def _():
                act(core)

    def out_copy(b, i, slot):
        if send:
            where = out.at[pl.ds(b * steps * tile + i * tile, tile), :]
        else:
            a = flags[COLUMN] if blocks[b] == 0 else 1 - flags[COLUMN]
            col = pl.multiple_of(flags[BASE2 if second else BASE1] + first_col, 128)
            where = out.at[a, pl.ds(i * tile, tile), pl.ds(col, width)]
        return pltpu.make_async_copy(obuf.at[slot], where, osem.at[slot])

    def exp_copy():
        return pltpu.make_async_copy(
            ecode, out.at[pl.ds(len(blocks) * steps * tile, EXPS), :], esem.at[0]
        )

    @pl.when(flags[CODED if send else RESULT] == 1)
    def _():
        def begin(core):
            for aux in range(2):
                col_copy(0, aux, 0 if send else core).start()
            for copy in row_copies(0, 0, core if send else 0):
                copy.start()
            for p in range(1, len(pieces)):
                for aux in range(2):
                    col_copy(p, aux, 0 if send else core).start()

        per_core(begin)
        if send:
            ebuf[...] = jnp.zeros_like(ebuf)
        for b in range(len(blocks)):

            def body(i, carry, b=b):
                def arrivals(core):
                    for step in range(steps):

                        @pl.when(i == step)
                        def _(step=step):
                            for copy in row_copies(b, step, core):
                                copy.wait()
                            if step + 1 < steps:
                                for copy in row_copies(b, step + 1, core):
                                    copy.start()
                            elif b + 1 < len(blocks):
                                for copy in row_copies(b + 1, 0, core):
                                    copy.start()

                if send:
                    per_core(arrivals)
                else:
                    arrivals(0)
                slot = lax.rem(i, 2)

                @pl.when(jnp.logical_or(b > 0, i >= 2))
                def _():
                    out_copy(b, i, slot).wait()

                for p, (off, n) in enumerate(pieces):
                    local = off - first_col
                    if b == 0:

                        @pl.when(i == 0)
                        def _(p=p):
                            for aux in range(2):
                                col_copy(p, aux, 0).wait()

                    acc = lax.dot_general(
                        rowbuf[b, pl.ds(pl.multiple_of(i * tile, 16), tile), :],
                        colbuf[pl.ds(local, n), :],
                        (((1,), (1,)), ((), ())),
                        preferred_element_type=jnp.float32,
                    )
                    if send:
                        code, exps = encode(acc, tile // GROUPS)
                        obuf[slot, :, pl.ds(local, n)] = code
                        for g in range(GROUPS):
                            ebuf[pl.ds((b * steps + i) * GROUPS + g, 1), pl.ds(local, n)] = exps[g]
                    else:
                        obuf[slot, :, pl.ds(local, n)] = acc
                out_copy(b, i, slot).start()
                return carry

            lax.fori_loop(0, steps, body, 0)
        if send:
            ecode[...] = ebuf[...].astype(jnp.int32).astype(jnp.int16)
            exp_copy().start()
        for slot in range(2):
            out_copy(len(blocks) - 1, slot, slot).wait()
        if send:
            exp_copy().wait()


TOKEN = (8, 128)


def mm_call(flags, token, send, chunks, blocks, row_arrays, second, which, col_arrays, out=None):
    width = sum(chunks[k][1] for k in which)
    depth = row_arrays[0][0][2][0][0].shape[1]
    block_rows = sum(n for _, n in chunks)
    tile = block_rows // TILES
    steps = TILES // 2 if send else TILES
    anywhere = pl.BlockSpec(memory_space=pltpu.HBM)
    operands = [flags, token]
    row_layout, col_layout = [], []
    for segments in row_arrays:
        row_layout.append([(off, size, tuple(b for _, b in halves)) for off, size, halves in segments])
        for _, _, halves in segments:
            operands += [array for array, _ in halves]
    for k in which:
        col_layout.append([tuple(b for _, b in source[k]) for source in col_arrays])
        for source in col_arrays:
            operands += [array for array, _ in source[k]]
    in_specs = [pl.BlockSpec(memory_space=pltpu.SMEM)]
    in_specs += [anywhere] * (len(operands) - 1)
    aliases = {}
    scratch = [
        pltpu.VMEM((len(blocks), steps * tile, 2 * depth), jnp.bfloat16),
        pltpu.VMEM((width, 2 * depth), jnp.bfloat16),
        pltpu.VMEM((2, tile, width), jnp.int16 if send else jnp.float32),
    ]
    sems = [
        pltpu.SemaphoreType.DMA((len(blocks), steps, 4, 2)),
        pltpu.SemaphoreType.DMA((len(which), 2)),
        pltpu.SemaphoreType.DMA((2,)),
    ]
    if send:
        out_shape = jax.ShapeDtypeStruct((len(blocks) * steps * tile + EXPS, width), jnp.int16)
        scratch += [pltpu.VMEM((EXPS, width), jnp.float32), pltpu.VMEM((EXPS, width), jnp.int16)]
        sems += [pltpu.SemaphoreType.DMA((1,))]
    else:
        out_shape = jax.ShapeDtypeStruct((2, block_rows, 2 * block_rows), jnp.float32)
        if out is not None:
            operands.append(out)
            in_specs.append(anywhere)
            aliases = {len(operands) - 1: 0}
    done = len(blocks) * steps * tile
    return pl.pallas_call(
        functools.partial(
            mm_kernel, send, chunks, blocks, second, which, row_layout, col_layout
        ),
        out_shape=(out_shape, jax.ShapeDtypeStruct(TOKEN, jnp.float32)),
        in_specs=in_specs,
        out_specs=(anywhere, pl.BlockSpec(memory_space=pltpu.VMEM)),
        scratch_shapes=scratch + sems,
        input_output_aliases=aliases,
        compiler_params=pltpu.CompilerParams(vmem_limit_bytes=VMEM_LIMIT),
        cost_estimate=pl.CostEstimate(flops=1, bytes_accessed=1, transcendentals=0),
        name="coded_tiles" if send else "result_tiles",
    )(*operands)


def decode_kernel(blocks, chunks, second, which, flags, _, code0, code1, out_in, out, token, qbuf, ebuf, obuf, qsem, esem, osem):
    block_rows = out.shape[1]
    tile = block_rows // TILES
    group = tile // GROUPS
    steps = TILES // 2
    width = sum(chunks[k][1] for k in which)
    first_col = chunks[which[0]][0]
    token[...] = jnp.zeros_like(token)

    @pl.when(flags[ARRIVE] == 1)
    def _():
        def in_copy(j, core, b, i):
            return pltpu.make_async_copy(
                (code0, code1)[core].at[pl.ds((b * steps + i) * tile, tile), :],
                qbuf.at[j],
                qsem.at[j],
            )

        def exp_copy(core):
            return pltpu.make_async_copy(
                (code0, code1)[core].at[pl.ds(len(blocks) * steps * tile, EXPS), :],
                ebuf.at[core],
                esem.at[core],
            )

        def out_copy(j, core, b, i):
            a = flags[COLUMN] if blocks[b] == 0 else 1 - flags[COLUMN]
            col = pl.multiple_of(flags[BASE2 if second else BASE1] + first_col, 128)
            return pltpu.make_async_copy(
                obuf.at[j % 2],
                out.at[a, pl.ds((core * steps + i) * tile, tile), pl.ds(col, width)],
                osem.at[j % 2],
            )

        work = [(core, b, i) for core in range(2) for b in range(len(blocks)) for i in range(steps)]
        for core in range(2):
            exp_copy(core).start()
        for j, item in enumerate(work):
            in_copy(j, *item).start()
        scales = []
        for core in range(2):
            exp_copy(core).wait()
            scales.append(jnp.exp2(ebuf[core].astype(jnp.int32).astype(jnp.float32) - 15.0))
        for j, item in enumerate(work):
            core, b, i = item
            in_copy(j, *item).wait()
            if j >= 2:
                out_copy(j - 2, *work[j - 2]).wait()
            values = qbuf[j].astype(jnp.int32).astype(jnp.float32)
            for g in range(GROUPS):
                pos = (b * steps + i) * GROUPS + g
                obuf[j % 2, pl.ds(g * group, group), :] = (
                    values[g * group : (g + 1) * group] * scales[core][pos : pos + 1]
                )
            out_copy(j, *item).start()
        for j in range(len(work) - 2, len(work)):
            out_copy(j, *work[j]).wait()


def decode_call(flags, token, coded, out, chunks, blocks, second, which):
    width = sum(chunks[k][1] for k in which)
    block_rows = out.shape[1]
    tile = block_rows // TILES
    count = TILES * len(blocks)
    anywhere = pl.BlockSpec(memory_space=pltpu.HBM)
    return pl.pallas_call(
        functools.partial(decode_kernel, blocks, chunks, second, which),
        out_shape=(
            jax.ShapeDtypeStruct(out.shape, out.dtype),
            jax.ShapeDtypeStruct(TOKEN, jnp.float32),
        ),
        in_specs=[pl.BlockSpec(memory_space=pltpu.SMEM)] + [anywhere] * 4,
        out_specs=(anywhere, pl.BlockSpec(memory_space=pltpu.VMEM)),
        scratch_shapes=[
            pltpu.VMEM((count, tile, width), jnp.int16),
            pltpu.VMEM((2, EXPS, width), jnp.int16),
            pltpu.VMEM((2, tile, width), jnp.float32),
            pltpu.SemaphoreType.DMA((count,)),
            pltpu.SemaphoreType.DMA((2,)),
            pltpu.SemaphoreType.DMA((2,)),
        ],
        input_output_aliases={4: 0},
        compiler_params=pltpu.CompilerParams(vmem_limit_bytes=VMEM_LIMIT),
        cost_estimate=pl.CostEstimate(flops=1, bytes_accessed=1, transcendentals=0),
        name="decode_tiles",
    )(flags, token, *coded, out)


def permute(value, move):
    pairs = []
    for r in range(4):
        for c in range(2):
            for s in range(2):
                to = move(r, c, s)
                if to is not None:
                    pairs.append(((r * 2 + c) * 2 + s, (to[0] * 2 + to[1]) * 2 + to[2]))
    return lax.ppermute(value, AXES, pairs)


def inner(r):
    return r in (1, 2)


def far_core(r):
    return 1 - r // 2


def symmetric_shards(chunks, orbital_factors, screen_mask):
    _, own_rows, occupied = orbital_factors.shape
    r, c, s = (lax.axis_index(name) for name in AXES)
    side = r // 2
    t = s ^ side
    inside = jnp.logical_and(r >= 1, r <= 2)
    near = t == 0
    flags = jnp.stack(
        [
            jnp.logical_or(near, inside).astype(jnp.int32),
            inside.astype(jnp.int32),
            jnp.logical_and(jnp.logical_not(near), jnp.logical_not(inside)).astype(jnp.int32),
            t.astype(jnp.int32),
            (jnp.where(near, 1 - r % 2, side) * own_rows).astype(jnp.int32),
            (jnp.where(near, r % 2, 1 - side) * own_rows).astype(jnp.int32),
            c.astype(jnp.int32),
            jnp.int32(0),
        ]
    )
    per_block = own_rows // BLK
    weights = lax.dynamic_slice(screen_mask, ((c * 4 + r) * per_block, s), (per_block, 1))
    weights = weights.astype(jnp.bfloat16)
    def mask(off, size):
        part = orbital_factors[0, off : off + size].reshape(size // BLK, BLK, occupied)
        part = part * weights[off // BLK : (off + size) // BLK][:, :, None]
        return part.reshape(size, occupied)

    outer_pair = lambda r, c, s: (r ^ 1, c, s)
    mid_pair = lambda r, c, s: (3 - r, c, s) if inner(r) else None
    x_pair = lambda r, c, s: (r, 1 - c, s)
    x_inner = lambda r, c, s: (r, 1 - c, s) if inner(r) else None
    swap = lambda r, c, s: (r, c, 1 - s)
    near_to_far = lambda r, c, s: (r ^ 1, c, 1 - s) if inner(r) and far_core(r) != s else None
    far_to_far = lambda r, c, s: (r ^ 1, c, s) if inner(r) and far_core(r) == s else None

    state = {"out": None, "token": jnp.zeros(TOKEN, jnp.float32)}
    arrays = {}
    moves = {
        "nb": outer_pair, "m1": mid_pair, "m2": mid_pair, "rx": x_pair, "nbx": x_inner,
        "n": near_to_far, "f": far_to_far,
    }
    sources = {"nb": "part", "m1": "part", "rx": "part", "m2": "nb", "nbx": "nb", "n": "code", "f": "code"}

    def tie(value):
        value, state["token"] = lax.optimization_barrier((value, state["token"]))
        return value

    def start(kind, k):
        arrays[kind, k] = permute(tie(arrays[sources[kind], k]), moves[kind])

    def done(kind, k):
        arrays[kind, k] = tie(arrays[kind, k])

    def start_swap(kind, k):
        arrays[kind + "_h", k] = permute(tie(arrays[kind, k]), swap)

    def done_swap(kind, k):
        arrays[kind + "_h", k] = tie(arrays[kind + "_h", k])

    def halves(kind, k, begin=0):
        return (arrays[kind, k], 0), (arrays[kind + "_h", k], begin)

    last = chunks[1][0], sum(size for _, size in chunks[1:])
    whole = 0, own_rows

    def row_segments(kind):
        if kind == "own":
            return [(*whole, halves("own", 0))]
        if kind == "rx":
            return [(*chunks[0], halves("rx", 0)), (*last, halves("rx", 1))]
        if kind == "nbx":
            first, *others = [(*chunk, k) for k, chunk in enumerate(chunks)]
            made = [(*first[:2], halves("nbx", 0))]
            for off, size, k in others:
                pair = (arrays["nbx", k], 0), (arrays["nbx2_h", 0], off - last[0])
                made.append((off, size, pair))
            return made
        return [(*chunk, halves(kind, k)) for k, chunk in enumerate(chunks)]

    def columns(kind, which):
        if kind == "own":
            (whole_o, _), (whole_h, _) = halves("own", 0)
            return {k: ((whole_o, chunks[k][0]), (whole_h, chunks[k][0])) for k in which}
        return {k: halves(kind, k) for k in which}

    everything = list(range(len(chunks)))

    def coded(name, blocks, second, which):
        rows = [row_segments(("nb", "nbx")[b]) for b in blocks]
        arrays["code", name], state["token"] = mm_call(
            flags, state["token"], True, chunks, blocks, rows, second, which,
            [columns(("m1", "m2")[second], which)],
        )
        arrays["item", name] = (blocks, second, which)

    def result(blocks, second, which):
        rows = [row_segments(("own", "rx")[b]) for b in blocks]
        cols = [columns(("nb", "own")[second], which), columns(("m1", "m2")[second], which)]
        state["out"], state["token"] = mm_call(
            flags, state["token"], False, chunks, blocks, rows, second, which, cols, state["out"]
        )

    def decode(name):
        state["out"], state["token"] = decode_call(
            flags, state["token"], [arrays["n", name], arrays["f", name]], state["out"], chunks,
            *arrays["item", name],
        )

    for k, (off, size) in enumerate(chunks):
        arrays["part", k] = mask(off, size)

    start("nb", 0)
    start("m1", 0)
    start("rx", 0)
    arrays["own", 0] = mask(*whole)
    start_swap("own", 0)
    done_swap("own", 0)
    done("nb", 0)
    done("m1", 0)
    done("rx", 0)
    start("nb", 1)
    start("m1", 1)
    start("nbx", 0)
    start_swap("nb", 0)
    start_swap("m1", 0)
    done_swap("nb", 0)
    done_swap("m1", 0)
    done("nb", 1)
    done("m1", 1)
    done("nbx", 0)
    start("nb", 2)
    start("m1", 2)
    start("nbx", 1)
    start_swap("nb", 1)
    start_swap("m1", 1)
    done_swap("nb", 1)
    done_swap("m1", 1)
    result((0,), 0, [0, 1])
    done("nb", 2)
    done("m1", 2)
    done("nbx", 1)
    start("m2", 1)
    start("nbx", 2)
    start_swap("nb", 2)
    start_swap("m1", 2)
    start_swap("nbx", 0)
    done_swap("nb", 2)
    done_swap("m1", 2)
    done_swap("nbx", 0)
    coded(0, (0,), 0, everything)
    start("n", 0)
    result((0,), 0, [2])
    done("m2", 1)
    done("nbx", 2)
    done("n", 0)
    start("m2", 2)
    start("f", 0)
    arrays["part", 1] = mask(*last)
    start("rx", 1)
    arrays["nbx2", 0] = jnp.concatenate([arrays["nbx", 1], arrays["nbx", 2]], axis=0)
    start_swap("m2", 1)
    start_swap("nbx2", 0)
    done_swap("m2", 1)
    done_swap("nbx2", 0)
    coded(1, (1,), 0, everything)
    done("f", 0)
    start("n", 1)
    coded(2, (0, 1), 1, [1])
    result((0,), 1, [1])
    done("m2", 2)
    done("n", 1)
    start("m2", 0)
    start("f", 1)
    start_swap("m2", 2)
    start_swap("rx", 0)
    done_swap("m2", 2)
    done_swap("rx", 0)
    coded(3, (0, 1), 1, [2])
    done("f", 1)
    start("n", 2)
    start("f", 2)
    result((0,), 1, [2])
    done("m2", 0)
    done("rx", 1)
    start_swap("m2", 0)
    start_swap("rx", 1)
    done_swap("m2", 0)
    done_swap("rx", 1)
    coded(4, (0, 1), 1, [0])
    done("n", 2)
    done("f", 2)
    start("n", 3)
    start("f", 3)
    decode(0)
    decode(1)
    result((0,), 1, [0])
    decode(2)
    result((1,), 0, everything)
    done("n", 3)
    done("f", 3)
    start("n", 4)
    start("f", 4)
    decode(3)
    result((1,), 1, everything)
    decode(4)
    return state["out"]


def split_rows(own_rows):
    units = own_rows // BLK
    sizes = [units // 3, (units + 1) // 3, (units + 2) // 3]
    chunks, off = [], 0
    for size in sizes:
        chunks.append((off * BLK, size * BLK))
        off += size
    return chunks


def solution(mesh):
    placed = (P("sub", ("groups", "col", "row"), None), P("groups", None))
    result = P(None, ("groups", "row"), ("col", "sub"))

    def shards(orbital_factors, screen_mask):
        aux_half, own_rows, _ = orbital_factors.shape
        small = (mesh.shape["row"], mesh.shape["col"], mesh.shape["sub"]) == (4, 2, 2)
        if small and aux_half == 1 and own_rows % (11 * BLK) == 0:
            return symmetric_shards(split_rows(own_rows), orbital_factors, screen_mask)
        return gathered_shards(orbital_factors, screen_mask)

    return jax.shard_map(
        shards, mesh=mesh, in_specs=placed, out_specs=result, check_vma=False
    )
```

```python
import functools

import jax
import jax.numpy as jnp
from jax import lax
from jax.experimental import pallas as pl
from jax.experimental.pallas import tpu as pltpu
from jax.sharding import PartitionSpec as P

BLK = 128
AXES = ("row", "col", "sub")
EXPS = 16
MAX_GROUP = 88
VMEM_LIMIT = 63 * 2**20
TOKEN = (8, 128)


def apply_screen(panel, first_row, screen_mask, aux_start):
    row_total = panel.shape[1]
    block_ids = (first_row + jnp.arange(row_total, dtype=jnp.int32)) // BLK
    one_hot = (
        block_ids[:, None] == jnp.arange(screen_mask.shape[0], dtype=jnp.int32)[None, :]
    ).astype(jnp.float32)
    row_weights = jnp.dot(
        one_hot, screen_mask.astype(jnp.float32), preferred_element_type=jnp.float32
    )
    row_weights = lax.dynamic_slice_in_dim(row_weights, aux_start, panel.shape[0], 1)
    return panel * jnp.transpose(row_weights).astype(jnp.bfloat16)[:, :, None]


def gathered_shards(orbital_factors, screen_mask):
    aux_half, own_rows, occupied = orbital_factors.shape
    row_count = lax.axis_size("row")
    col_count = lax.axis_size("col")
    row_pos = lax.axis_index("row")
    col_pos = lax.axis_index("col")
    sub_pos = lax.axis_index("sub")
    own_first = (col_pos * row_count + row_pos) * own_rows
    screened = apply_screen(orbital_factors, own_first, screen_mask, sub_pos * aux_half)
    contract_dims = (((0, 2), (0, 2)), ((), ()))
    gathered_rows = lax.all_gather(screened, "col", axis=1, tiled=True)
    partial_tile = lax.dot_general(
        gathered_rows,
        lax.all_gather(screened, "row", axis=1, tiled=True),
        contract_dims,
        preferred_element_type=jnp.float32,
    )
    tile_sum = lax.psum_scatter(partial_tile, "sub", scatter_dimension=1, tiled=True)
    return tile_sum.reshape(col_count, own_rows, tile_sum.shape[1])


RESULT, CODED, ARRIVE, FAR, BASE1, BASE2, COLUMN = range(7)


def encode(acc, group):
    coded, exps = [], []
    for first in range(0, acc.shape[0], group):
        part = acc[first : first + group]
        top = jnp.max(jnp.abs(part), axis=0, keepdims=True)
        exp = jnp.floor(jnp.log2(jnp.maximum(top, 2.0**-100))) + 1.0
        scaled = jnp.round(part * jnp.exp2(15.0 - exp))
        coded.append(jnp.clip(scaled, -32767.0, 32767.0).astype(jnp.int32))
        exps.append(exp)
    return jnp.concatenate(coded, axis=0).astype(jnp.int16), exps


class Rows:
    def __init__(self, block, lo, count, send):
        self.block, self.lo, self.count = block, lo, count
        self.mine = count // 2 if send else count
        self.steps = 2 if send or count % 1408 else 4
        self.tile = self.mine // self.steps
        self.group = max(g for g in range(8, MAX_GROUP + 1, 8) if self.tile % g == 0)


def overlap(segments, lo, hi):
    parts = []
    for k, (off, size) in enumerate(segments):
        first, last = max(lo, off), min(hi, off + size)
        if first < last:
            parts.append((k, first - off, last - first, first - lo))
    return parts


def target(flags, out, rows, lo, count, second, col, width):
    a = flags[COLUMN] if rows.block == 0 else 1 - flags[COLUMN]
    base = pl.multiple_of(flags[BASE2 if second else BASE1] + col, 128)
    return out.at[a, pl.ds(lo, count), pl.ds(base, width)]


def groups_of(send, blocks, pieces):
    if not send and len(blocks) == 1:
        return [(0, [p]) for p in range(len(pieces))]
    return [(b, list(range(len(pieces)))) for b in range(len(blocks))]


def locals_of(pieces):
    return [sum(n for _, _, n in pieces[:p]) for p in range(len(pieces))]


def mm_kernel(send, blocks, pieces, row_layout, col_layout, *refs):
    it = iter(refs)
    flags = next(it)
    next(it)
    rows = [[[next(it) for _ in range(2)] for _ in segments] for segments in row_layout]
    cols = [[[next(it) for _ in range(2)] for _ in sources] for sources in col_layout]
    rest = list(it)
    if send:
        out, token, rowbuf, colbuf, obuf, ebuf, ecode, rsem, csem, osem, esem = rest
    else:
        out, token, rowbuf, colbuf, obuf, rsem, csem, osem = rest[-8:]
    depth = rows[0][0][0].shape[1]
    begins = locals_of(pieces)
    firsts = [sum(r.mine for r in blocks[:b]) for b in range(len(blocks))]
    total = sum(r.mine for r in blocks)
    groups = groups_of(send, blocks, pieces)
    token[...] = jnp.zeros_like(token)

    def col_copy(p, aux, core):
        size = pieces[p][2]
        return pltpu.make_async_copy(
            cols[p][core][aux].at[pl.ds(col_layout[p][core][aux], size), :],
            colbuf.at[pl.ds(begins[p], size), pl.ds(aux * depth, depth)],
            csem.at[p, aux],
        )

    def row_copies(b, i, core):
        r = blocks[b]
        lo = r.lo + core * r.mine + i * r.tile
        spans = [(off, size) for off, size, _ in row_layout[b]]
        made = []
        for j, (k, off, size, local) in enumerate(overlap(spans, lo, lo + r.tile)):
            for aux in range(2):
                made.append(
                    pltpu.make_async_copy(
                        rows[b][k][aux].at[pl.ds(row_layout[b][k][2][aux] + off, size), :],
                        rowbuf.at[
                            pl.ds(firsts[b] + i * r.tile + local, size), pl.ds(aux * depth, depth)
                        ],
                        rsem.at[b, i, j, aux],
                    )
                )
        return made

    def per_core(act):
        for core in range(2):

            @pl.when(flags[FAR] == core)
            def _():
                act(core)

    def out_copies(g, i, slot):
        b, members = groups[g]
        r = blocks[b]
        if send:
            where = out.at[pl.ds(firsts[b] + i * r.tile, r.tile), :]
            return [pltpu.make_async_copy(obuf.at[slot, pl.ds(0, r.tile), :], where, osem.at[slot, 0])]
        made = []
        for p in members:
            second, off, n = pieces[p]
            where = target(flags, out, r, r.lo + i * r.tile, r.tile, second, off, n)
            source = obuf.at[slot, pl.ds(0, r.tile), pl.ds(begins[p] - begins[members[0]], n)]
            made.append(pltpu.make_async_copy(source, where, osem.at[slot, p]))
        return made

    def out_start(g, i, slot):
        for copy in out_copies(g, i, slot):
            copy.start()

    def out_wait(g, i, slot):
        for copy in out_copies(g, i, slot):
            copy.wait()

    def exp_copy():
        return pltpu.make_async_copy(ecode, out.at[pl.ds(total, EXPS), :], esem.at[0])

    @pl.when(flags[CODED if send else RESULT] == 1)
    def _():
        def load(j):
            def begin(core):
                for aux in range(2):
                    col_copy(j, aux, 0 if send else core).start()

            if send:
                begin(0)
            else:
                per_core(begin)

        def load_rows(b, step):
            def begin(core):
                for copy in row_copies(b, step, core):
                    copy.start()

            if send:
                per_core(begin)
            else:
                begin(0)

        def wait_rows(b, step):
            def arrive(core):
                for copy in row_copies(b, step, core):
                    copy.wait()

            if send:
                per_core(arrive)
            else:
                arrive(0)

        def load_next(b, step):
            if step + 1 < blocks[b].steps:
                load_rows(b, step + 1)
            elif b + 1 < len(blocks):
                load_rows(b + 1, 0)

        def multiply(b, i, slot, local, size, place, scales):
            r = blocks[b]
            acc = lax.dot_general(
                rowbuf[pl.ds(pl.multiple_of(firsts[b] + i * r.tile, 16), r.tile), :],
                colbuf[pl.ds(local, size), :],
                (((1,), (1,)), ((), ())),
                preferred_element_type=jnp.float32,
            )
            if send:
                acc, exps = encode(acc, r.group)
                for g, exp in enumerate(exps):
                    pos = scales + i * (r.tile // r.group) + g
                    ebuf[pl.ds(pos, 1), pl.ds(local, size)] = exp
            obuf[slot, pl.ds(0, r.tile), pl.ds(place, size)] = acc

        load(0)
        load_rows(0, 0)
        for p in range(1, len(groups[0][1])):
            load(p)
        if send:
            ebuf[...] = jnp.zeros_like(ebuf)
        scales = 0
        for g, (b, members) in enumerate(groups):
            r = blocks[b]
            new_rows = g == 0 or groups[g - 1][0] != b
            new_cols = [p for p in members if all(p not in group[1] for group in groups[:g])]

            def body(i, carry, g=g, b=b, r=r, members=members, new_rows=new_rows, new_cols=new_cols, scales=scales):
                if new_rows:
                    for step in range(r.steps):

                        @pl.when(i == step)
                        def _(step=step):
                            wait_rows(b, step)
                            load_next(b, step)

                slot = lax.rem(i, 2)

                @pl.when(i >= 2)
                def _():
                    out_wait(g, i - 2, slot)

                if g > 0:

                    @pl.when(i < 2)
                    def _():
                        out_wait(g - 1, blocks[groups[g - 1][0]].steps - 2 + i, slot)

                for p in members:
                    if p in new_cols:

                        @pl.when(i == 0)
                        def _(p=p):
                            for aux in range(2):
                                col_copy(p, aux, 0).wait()
                            if g + 1 < len(groups) and p == new_cols[-1]:
                                for later in groups[g + 1][1]:
                                    if later not in members:
                                        load(later)

                    multiply(b, i, slot, begins[p], pieces[p][2], begins[p] - begins[members[0]], scales)
                out_start(g, i, slot)
                return carry

            lax.fori_loop(0, r.steps, body, 0)
            scales += r.mine // r.group
        if send:
            ecode[...] = ebuf[...].astype(jnp.int32).astype(jnp.int16)
            exp_copy().start()
        for slot in range(2):
            out_wait(len(groups) - 1, blocks[-1].steps - 2 + slot, slot)
        if send:
            exp_copy().wait()


def mm_call(flags, token, send, blocks, row_arrays, pieces, col_arrays, out, own_rows):
    width = sum(n for _, _, n in pieces)
    depth = row_arrays[0][0][2][0][0].shape[1]
    total = sum(r.mine for r in blocks)
    tile = max(r.tile for r in blocks)
    held = max(sum(pieces[p][2] for p in ps) for _, ps in groups_of(send, blocks, pieces))
    anywhere = pl.BlockSpec(memory_space=pltpu.HBM)
    operands = [flags, token]
    row_layout, col_layout = [], []
    for segments in row_arrays:
        row_layout.append([(off, size, tuple(b for _, b in halves)) for off, size, halves in segments])
        for _, _, halves in segments:
            operands += [array for array, _ in halves]
    for sources in col_arrays:
        col_layout.append([tuple(b for _, b in source) for source in sources])
        for source in sources:
            operands += [array for array, _ in source]
    in_specs = [pl.BlockSpec(memory_space=pltpu.SMEM)]
    in_specs += [anywhere] * (len(operands) - 1)
    aliases = {}
    scratch = [
        pltpu.VMEM((total, 2 * depth), jnp.bfloat16),
        pltpu.VMEM((width, 2 * depth), jnp.bfloat16),
        pltpu.VMEM((2, tile, held), jnp.int16 if send else jnp.float32),
    ]
    sems = [
        pltpu.SemaphoreType.DMA((len(blocks), max(r.steps for r in blocks), 4, 2)),
        pltpu.SemaphoreType.DMA((len(pieces), 2)),
        pltpu.SemaphoreType.DMA((2, len(pieces))),
    ]
    if send:
        out_shape = jax.ShapeDtypeStruct((total + EXPS, width), jnp.int16)
        scratch += [pltpu.VMEM((EXPS, width), jnp.float32), pltpu.VMEM((EXPS, width), jnp.int16)]
        sems += [pltpu.SemaphoreType.DMA((1,))]
    else:
        out_shape = jax.ShapeDtypeStruct((2, own_rows, 2 * own_rows), jnp.float32)
        if out is not None:
            operands.append(out)
            in_specs.append(anywhere)
            aliases = {len(operands) - 1: 0}
    return pl.pallas_call(
        functools.partial(mm_kernel, send, blocks, pieces, row_layout, col_layout),
        out_shape=(out_shape, jax.ShapeDtypeStruct(TOKEN, jnp.float32)),
        in_specs=in_specs,
        out_specs=(anywhere, pl.BlockSpec(memory_space=pltpu.VMEM)),
        scratch_shapes=scratch + sems,
        input_output_aliases=aliases,
        compiler_params=pltpu.CompilerParams(vmem_limit_bytes=VMEM_LIMIT),
        cost_estimate=pl.CostEstimate(flops=1, bytes_accessed=1, transcendentals=0),
        name="coded_tiles" if send else "result_tiles",
    )(*operands)


def decode_kernel(blocks, pieces, *refs):
    flags, _, code0, code1, _, out, token, qbuf, ebuf, obuf, qsem, esem, osem = refs
    width = sum(n for _, _, n in pieces)
    total = sum(r.mine for r in blocks)
    token[...] = jnp.zeros_like(token)
    work = []
    for core in range(2):
        row, scale = 0, 0
        for r in blocks:
            for i in range(r.steps):
                work.append((core, r, row, r.lo + core * r.mine + i * r.tile, scale))
                row += r.tile
                scale += r.tile // r.group

    @pl.when(flags[ARRIVE] == 1)
    def _():
        def in_copy(j):
            core, r, row, _, _ = work[j]
            return pltpu.make_async_copy(
                (code0, code1)[core].at[pl.ds(row, r.tile), :],
                qbuf.at[j, pl.ds(0, r.tile), :],
                qsem.at[j],
            )

        def exp_copy(core):
            return pltpu.make_async_copy(
                (code0, code1)[core].at[pl.ds(total, EXPS), :], ebuf.at[core], esem.at[core]
            )

        def out_copy(j):
            _, r, _, lo, _ = work[j]
            return pltpu.make_async_copy(
                obuf.at[j % 2, pl.ds(0, r.tile), :],
                target(flags, out, r, lo, r.tile, *pieces[0][:2], width),
                osem.at[j % 2],
            )

        for core in range(2):
            exp_copy(core).start()
        for j in range(len(work)):
            in_copy(j).start()
        scales = []
        for core in range(2):
            exp_copy(core).wait()
            scales.append(jnp.exp2(ebuf[core].astype(jnp.int32).astype(jnp.float32) - 15.0))
        for j, (core, r, _, _, scale) in enumerate(work):
            in_copy(j).wait()
            if j >= 2:
                out_copy(j - 2).wait()
            values = qbuf[j, pl.ds(0, r.tile), :].astype(jnp.int32).astype(jnp.float32)
            for g in range(r.tile // r.group):
                obuf[j % 2, pl.ds(g * r.group, r.group), :] = (
                    values[g * r.group : (g + 1) * r.group] * scales[core][scale + g : scale + g + 1]
                )
            out_copy(j).start()
        for j in range(len(work) - 2, len(work)):
            out_copy(j).wait()


def decode_call(flags, token, coded, out, blocks, pieces):
    width = sum(n for _, _, n in pieces)
    tile = max(r.tile for r in blocks)
    count = 2 * sum(r.steps for r in blocks)
    anywhere = pl.BlockSpec(memory_space=pltpu.HBM)
    return pl.pallas_call(
        functools.partial(decode_kernel, blocks, pieces),
        out_shape=(
            jax.ShapeDtypeStruct(out.shape, out.dtype),
            jax.ShapeDtypeStruct(TOKEN, jnp.float32),
        ),
        in_specs=[pl.BlockSpec(memory_space=pltpu.SMEM)] + [anywhere] * 4,
        out_specs=(anywhere, pl.BlockSpec(memory_space=pltpu.VMEM)),
        scratch_shapes=[
            pltpu.VMEM((count, tile, width), jnp.int16),
            pltpu.VMEM((2, EXPS, width), jnp.int16),
            pltpu.VMEM((2, tile, width), jnp.float32),
            pltpu.SemaphoreType.DMA((count,)),
            pltpu.SemaphoreType.DMA((2,)),
            pltpu.SemaphoreType.DMA((2,)),
        ],
        input_output_aliases={4: 0},
        compiler_params=pltpu.CompilerParams(vmem_limit_bytes=VMEM_LIMIT),
        cost_estimate=pl.CostEstimate(flops=1, bytes_accessed=1, transcendentals=0),
        name="decode_tiles",
    )(flags, token, *coded, out)


def permute(value, move):
    pairs = []
    for r in range(4):
        for c in range(2):
            for s in range(2):
                to = move(r, c, s)
                if to is not None:
                    pairs.append(((r * 2 + c) * 2 + s, (to[0] * 2 + to[1]) * 2 + to[2]))
    return lax.ppermute(value, AXES, pairs)


def inner(r):
    return r in (1, 2)


def far_core(r):
    return 1 - r // 2


def symmetric_shards(chunks, orbital_factors, screen_mask):
    _, own_rows, occupied = orbital_factors.shape
    r, c, s = (lax.axis_index(name) for name in AXES)
    side = r // 2
    t = s ^ side
    inside = jnp.logical_and(r >= 1, r <= 2)
    near = t == 0
    flags = jnp.stack(
        [
            jnp.logical_or(near, inside).astype(jnp.int32),
            inside.astype(jnp.int32),
            jnp.logical_and(jnp.logical_not(near), jnp.logical_not(inside)).astype(jnp.int32),
            t.astype(jnp.int32),
            (jnp.where(near, 1 - r % 2, side) * own_rows).astype(jnp.int32),
            (jnp.where(near, r % 2, 1 - side) * own_rows).astype(jnp.int32),
            c.astype(jnp.int32),
            jnp.int32(0),
        ]
    )
    per_block = own_rows // BLK
    weights = lax.dynamic_slice(screen_mask, ((c * 4 + r) * per_block, s), (per_block, 1))
    weights = weights.astype(jnp.bfloat16)
    def mask(off, size):
        part = orbital_factors[0, off : off + size].reshape(size // BLK, BLK, occupied)
        part = part * weights[off // BLK : (off + size) // BLK][:, :, None]
        return part.reshape(size, occupied)

    outer_pair = lambda r, c, s: (r ^ 1, c, s)
    mid_pair = lambda r, c, s: (3 - r, c, s) if inner(r) else None
    x_pair = lambda r, c, s: (r, 1 - c, s)
    x_inner = lambda r, c, s: (r, 1 - c, s) if inner(r) else None
    swap = lambda r, c, s: (r, c, 1 - s)
    near_to_far = lambda r, c, s: (r ^ 1, c, 1 - s) if inner(r) and far_core(r) != s else None
    far_to_far = lambda r, c, s: (r ^ 1, c, s) if inner(r) and far_core(r) == s else None

    state = {"out": None, "token": jnp.zeros(TOKEN, jnp.float32)}
    arrays = {}
    moves = {
        "nb": outer_pair, "m1": mid_pair, "m2": mid_pair, "rx": x_pair, "nbx": x_inner,
        "n": near_to_far, "f": far_to_far,
    }
    sources = {"nb": "part", "m1": "part", "rx": "part", "m2": "nb", "nbx": "nb", "n": "code", "f": "code"}

    def tie(value):
        value, state["token"] = lax.optimization_barrier((value, state["token"]))
        return value

    def start(kind, k):
        arrays[kind, k] = permute(tie(arrays[sources[kind], k]), moves[kind])

    def done(kind, k):
        arrays[kind, k] = tie(arrays[kind, k])

    def start_swap(kind, k):
        arrays[kind + "_h", k] = permute(tie(arrays[kind, k]), swap)

    def done_swap(kind, k):
        arrays[kind + "_h", k] = tie(arrays[kind + "_h", k])

    first, last = chunks

    def halves(kind, k):
        if (kind + "_h", k) in arrays:
            other = arrays[kind + "_h", k], 0
        else:
            other = arrays["pack_h", 0], {"m1": 0, "rx": first[1]}[kind]
        return (arrays[kind, k], 0), other

    def rows_of(kinds, send):
        blocks, segments = [], []
        for kind, which in kinds:
            lo = chunks[which[0]][0]
            count = sum(chunks[k][1] for k in which)
            blocks.append(Rows(int(kind in ("nbx", "rx")), lo, count, send))
            segments.append([(*chunks[k], halves(kind, k)) for k in which])
        return blocks, segments

    def pieces_of(where):
        return [(second, *chunks[k]) for second, k in where]

    def coded(name, kinds, *where):
        blocks, rows = rows_of(kinds, True)
        cols = [[halves(("m1", "m2")[second], k)] for second, k in where]
        arrays["code", name], state["token"] = mm_call(
            flags, state["token"], True, blocks, rows, pieces_of(where), cols, None, own_rows
        )
        arrays["item", name] = (blocks, pieces_of(where))

    def result(kinds, *where):
        blocks, rows = rows_of(kinds, False)
        names = (("nb", "m1"), ("own", "m2"))
        cols = [[halves(kind, k) for kind in names[second]] for second, k in where]
        state["out"], state["token"] = mm_call(
            flags, state["token"], False, blocks, rows, pieces_of(where), cols, state["out"], own_rows
        )

    def decode(name):
        state["out"], state["token"] = decode_call(
            flags, state["token"], [arrays["n", name], arrays["f", name]], state["out"],
            *arrays["item", name],
        )

    for k, chunk in enumerate(chunks):
        arrays["part", k] = arrays["own", k] = mask(*chunk)
    both = [0, 1]

    start("nb", 0)
    start("m1", 0)
    start("rx", 0)
    start_swap("own", 0)
    start_swap("own", 1)
    done_swap("own", 0)
    done_swap("own", 1)
    done("nb", 0)
    done("m1", 0)
    done("rx", 0)
    start("nb", 1)
    start("m1", 1)
    start("nbx", 0)
    arrays["pack", 0] = jnp.concatenate([arrays["m1", 0], arrays["rx", 0]], axis=0)
    start_swap("nb", 0)
    start_swap("pack", 0)
    done_swap("nb", 0)
    done_swap("pack", 0)
    result([("own", both), ("rx", [0])], (0, 0))
    done("nb", 1)
    done("m1", 1)
    done("nbx", 0)
    start("m2", 1)
    start("nbx", 1)
    start_swap("nb", 1)
    start_swap("m1", 1)
    start_swap("nbx", 0)
    done_swap("nb", 1)
    done_swap("m1", 1)
    done_swap("nbx", 0)
    coded(0, [("nb", both)], (0, 0), (0, 1))
    start("n", 0)
    start("f", 0)
    coded(1, [("nbx", [0])], (0, 0), (0, 1))
    result([("own", both), ("rx", [0])], (0, 1))
    done("m2", 1)
    done("nbx", 1)
    done("n", 0)
    done("f", 0)
    start("m2", 0)
    start("n", 1)
    start("f", 1)
    start_swap("m2", 1)
    start_swap("nbx", 1)
    done_swap("m2", 1)
    done_swap("nbx", 1)
    start("rx", 1)
    coded(2, [("nbx", [1])], (0, 0), (0, 1))
    done("n", 1)
    done("f", 1)
    start("n", 2)
    start("f", 2)
    coded(3, [("nb", both), ("nbx", both)], (1, 1))
    done("m2", 0)
    done("n", 2)
    done("f", 2)
    start("n", 3)
    start("f", 3)
    start_swap("m2", 0)
    done_swap("m2", 0)
    coded(4, [("nb", both), ("nbx", both)], (1, 0))
    result([("own", both), ("rx", [0])], (1, 1))
    done("n", 3)
    done("f", 3)
    start("n", 4)
    start("f", 4)
    done("rx", 1)
    start_swap("rx", 1)
    for name in range(4):
        decode(name)
    result([("own", both), ("rx", [0])], (1, 0))
    done_swap("rx", 1)
    result([("rx", [1])], (0, 0), (0, 1), (1, 1), (1, 0))
    decode(4)
    return state["out"]


def split_rows(own_rows):
    size = own_rows // BLK // 2 * BLK
    return [(0, size), (size, own_rows - size)]


def solution(mesh):
    placed = (P("sub", ("groups", "col", "row"), None), P("groups", None))
    result = P(None, ("groups", "row"), ("col", "sub"))

    def shards(orbital_factors, screen_mask):
        aux_half, own_rows, _ = orbital_factors.shape
        small = (mesh.shape["row"], mesh.shape["col"], mesh.shape["sub"]) == (4, 2, 2)
        if small and aux_half == 1 and own_rows == 11 * BLK:
            return symmetric_shards(split_rows(own_rows), orbital_factors, screen_mask)
        return gathered_shards(orbital_factors, screen_mask)

    return jax.shard_map(
        shards, mesh=mesh, in_specs=placed, out_specs=result, check_vma=False
    )
```

```python
import functools

import jax
import jax.numpy as jnp
from jax import lax
from jax.experimental import pallas as pl
from jax.experimental.pallas import tpu as pltpu
from jax.sharding import PartitionSpec as P

BLK = 128
AXES = ("row", "col", "sub")
MAX_GROUP = 88
VMEM_LIMIT = 63 * 2**20
TOKEN = (8, 128)


def apply_screen(panel, first_row, screen_mask, aux_start):
    row_total = panel.shape[1]
    block_ids = (first_row + jnp.arange(row_total, dtype=jnp.int32)) // BLK
    one_hot = (
        block_ids[:, None] == jnp.arange(screen_mask.shape[0], dtype=jnp.int32)[None, :]
    ).astype(jnp.float32)
    row_weights = jnp.dot(
        one_hot, screen_mask.astype(jnp.float32), preferred_element_type=jnp.float32
    )
    row_weights = lax.dynamic_slice_in_dim(row_weights, aux_start, panel.shape[0], 1)
    return panel * jnp.transpose(row_weights).astype(jnp.bfloat16)[:, :, None]


def gathered_shards(orbital_factors, screen_mask):
    aux_half, own_rows, occupied = orbital_factors.shape
    row_count = lax.axis_size("row")
    col_count = lax.axis_size("col")
    row_pos = lax.axis_index("row")
    col_pos = lax.axis_index("col")
    sub_pos = lax.axis_index("sub")
    own_first = (col_pos * row_count + row_pos) * own_rows
    screened = apply_screen(orbital_factors, own_first, screen_mask, sub_pos * aux_half)
    contract_dims = (((0, 2), (0, 2)), ((), ()))
    gathered_rows = lax.all_gather(screened, "col", axis=1, tiled=True)
    partial_tile = lax.dot_general(
        gathered_rows,
        lax.all_gather(screened, "row", axis=1, tiled=True),
        contract_dims,
        preferred_element_type=jnp.float32,
    )
    tile_sum = lax.psum_scatter(partial_tile, "sub", scatter_dimension=1, tiled=True)
    return tile_sum.reshape(col_count, own_rows, tile_sum.shape[1])


RESULT, CODED, ARRIVE, FAR, BASE1, BASE2, COLUMN, NEAR, FAR_INSIDE, CODED_NEAR = range(10)


def encode(acc, group):
    coded, exps = [], []
    for first in range(0, acc.shape[0], group):
        part = acc[first : first + group]
        top = jnp.max(jnp.abs(part), axis=0, keepdims=True)
        exp = jnp.floor(jnp.log2(jnp.maximum(top, 2.0**-100))) + 1.0
        scaled = jnp.round(part * jnp.exp2(15.0 - exp))
        coded.append(jnp.clip(scaled, -32767.0, 32767.0).astype(jnp.int32))
        exps.append(exp)
    return jnp.concatenate(coded, axis=0).astype(jnp.int16), exps


class Rows:
    def __init__(self, block, lo, count, cores):
        self.block, self.lo, self.count = block, lo, count
        self.mine = count // cores
        self.steps = 2 if self.mine < 1024 else 4
        self.tile = self.mine // self.steps
        self.group = max(g for g in range(8, MAX_GROUP + 1, 8) if self.tile % g == 0)


def exponent_rows(blocks):
    return -(-sum(r.mine // r.group for r in blocks) // 16) * 16


def overlap(segments, lo, hi):
    parts = []
    for k, (off, size) in enumerate(segments):
        first, last = max(lo, off), min(hi, off + size)
        if first < last:
            parts.append((k, first - off, last - first, first - lo))
    return parts


def target(flags, out, rows, lo, count, second, col, width):
    a = flags[COLUMN] if rows.block == 0 else 1 - flags[COLUMN]
    base = pl.multiple_of(flags[BASE2 if second else BASE1] + col, 128)
    return out.at[a, pl.ds(lo, count), pl.ds(base, width)]


def groups_of(send, blocks, pieces):
    if not send and len(blocks) == 1:
        return [(0, [p]) for p in range(len(pieces))]
    return [(b, list(range(len(pieces)))) for b in range(len(blocks))]


def locals_of(pieces):
    return [sum(n for _, _, n in pieces[:p]) for p in range(len(pieces))]


def mm_kernel(send, active, blocks, pieces, row_layout, col_layout, *refs):
    it = iter(refs)
    flags = next(it)
    next(it)
    rows = [[[next(it) for _ in range(2)] for _ in segments] for segments in row_layout]
    cols = [[[next(it) for _ in range(2)] for _ in sources] for sources in col_layout]
    rest = list(it)
    if send:
        out, token, rowbuf, colbuf, obuf, ebuf, ecode, rsem, csem, osem, esem = rest
    else:
        out, token, rowbuf, colbuf, obuf, rsem, csem, osem = rest[-8:]
    depth = rows[0][0][0].shape[1]
    begins = locals_of(pieces)
    firsts = [sum(r.mine for r in blocks[:b]) for b in range(len(blocks))]
    total = sum(r.mine for r in blocks)
    groups = groups_of(send, blocks, pieces)
    token[...] = jnp.zeros_like(token)

    def col_copy(p, aux, core):
        size = pieces[p][2]
        return pltpu.make_async_copy(
            cols[p][core][aux].at[pl.ds(col_layout[p][core][aux], size), :],
            colbuf.at[pl.ds(begins[p], size), pl.ds(aux * depth, depth)],
            csem.at[p, aux],
        )

    def row_copies(b, i, core):
        r = blocks[b]
        lo = r.lo + core * r.mine + i * r.tile
        spans = [(off, size) for off, size, _ in row_layout[b]]
        made = []
        for j, (k, off, size, local) in enumerate(overlap(spans, lo, lo + r.tile)):
            for aux in range(2):
                made.append(
                    pltpu.make_async_copy(
                        rows[b][k][aux].at[pl.ds(row_layout[b][k][2][aux] + off, size), :],
                        rowbuf.at[
                            pl.ds(firsts[b] + i * r.tile + local, size), pl.ds(aux * depth, depth)
                        ],
                        rsem.at[b, i, j, aux],
                    )
                )
        return made

    def per_core(act):
        for core in range(2):

            @pl.when(flags[FAR] == core)
            def _():
                act(core)

    def out_copies(g, i, slot):
        b, members = groups[g]
        r = blocks[b]
        if send:
            where = out.at[pl.ds(firsts[b] + i * r.tile, r.tile), :]
            return [pltpu.make_async_copy(obuf.at[slot, pl.ds(0, r.tile), :], where, osem.at[slot, 0])]
        made = []
        for p in members:
            second, off, n = pieces[p]
            where = target(flags, out, r, r.lo + i * r.tile, r.tile, second, off, n)
            source = obuf.at[slot, pl.ds(0, r.tile), pl.ds(begins[p] - begins[members[0]], n)]
            made.append(pltpu.make_async_copy(source, where, osem.at[slot, p]))
        return made

    def out_start(g, i, slot):
        for copy in out_copies(g, i, slot):
            copy.start()

    def out_wait(g, i, slot):
        for copy in out_copies(g, i, slot):
            copy.wait()

    def exp_copy():
        return pltpu.make_async_copy(
            ecode, out.at[pl.ds(total, exponent_rows(blocks)), :], esem.at[0]
        )

    @pl.when(flags[active] == 1)
    def _():
        def load(j):
            def begin(core):
                for aux in range(2):
                    col_copy(j, aux, core if len(cols[j]) > 1 else 0).start()

            if len(cols[j]) > 1:
                per_core(begin)
            else:
                begin(0)

        def load_rows(b, step):
            def begin(core):
                for copy in row_copies(b, step, core):
                    copy.start()

            if send:
                per_core(begin)
            else:
                begin(0)

        def wait_rows(b, step):
            def arrive(core):
                for copy in row_copies(b, step, core):
                    copy.wait()

            if send:
                per_core(arrive)
            else:
                arrive(0)

        def load_next(b, step):
            if step + 1 < blocks[b].steps:
                load_rows(b, step + 1)
            elif b + 1 < len(blocks):
                load_rows(b + 1, 0)

        def multiply(b, i, slot, local, size, place, scales):
            r = blocks[b]
            acc = lax.dot_general(
                rowbuf[pl.ds(pl.multiple_of(firsts[b] + i * r.tile, 16), r.tile), :],
                colbuf[pl.ds(local, size), :],
                (((1,), (1,)), ((), ())),
                preferred_element_type=jnp.float32,
            )
            if send:
                acc, exps = encode(acc, r.group)
                for g, exp in enumerate(exps):
                    pos = scales + i * (r.tile // r.group) + g
                    ebuf[pl.ds(pos, 1), pl.ds(local, size)] = exp
            obuf[slot, pl.ds(0, r.tile), pl.ds(place, size)] = acc

        load(0)
        load_rows(0, 0)
        for p in range(1, len(groups[0][1])):
            load(p)
        if send:
            ebuf[...] = jnp.zeros_like(ebuf)
        scales = 0
        for g, (b, members) in enumerate(groups):
            r = blocks[b]
            new_rows = g == 0 or groups[g - 1][0] != b
            new_cols = [p for p in members if all(p not in group[1] for group in groups[:g])]

            def body(i, carry, g=g, b=b, r=r, members=members, new_rows=new_rows, new_cols=new_cols, scales=scales):
                if new_rows:
                    for step in range(r.steps):

                        @pl.when(i == step)
                        def _(step=step):
                            wait_rows(b, step)
                            load_next(b, step)

                slot = lax.rem(i, 2)

                @pl.when(i >= 2)
                def _():
                    out_wait(g, i - 2, slot)

                if g > 0:

                    @pl.when(i < 2)
                    def _():
                        out_wait(g - 1, blocks[groups[g - 1][0]].steps - 2 + i, slot)

                for p in members:
                    if p in new_cols:

                        @pl.when(i == 0)
                        def _(p=p):
                            for aux in range(2):
                                col_copy(p, aux, 0).wait()
                            if g + 1 < len(groups) and p == new_cols[-1]:
                                for later in groups[g + 1][1]:
                                    if later not in members:
                                        load(later)

                    multiply(b, i, slot, begins[p], pieces[p][2], begins[p] - begins[members[0]], scales)
                out_start(g, i, slot)
                return carry

            lax.fori_loop(0, r.steps, body, 0)
            scales += r.mine // r.group
        if send:
            ecode[...] = ebuf[...].astype(jnp.int32).astype(jnp.int16)
            exp_copy().start()
        for slot in range(2):
            out_wait(len(groups) - 1, blocks[-1].steps - 2 + slot, slot)
        if send:
            exp_copy().wait()


def mm_call(flags, token, send, active, blocks, row_arrays, pieces, col_arrays, out, own_rows):
    width = sum(n for _, _, n in pieces)
    depth = row_arrays[0][0][2][0][0].shape[1]
    total = sum(r.mine for r in blocks)
    tile = max(r.tile for r in blocks)
    held = max(sum(pieces[p][2] for p in ps) for _, ps in groups_of(send, blocks, pieces))
    anywhere = pl.BlockSpec(memory_space=pltpu.HBM)
    operands = [flags, token]
    row_layout, col_layout = [], []
    for segments in row_arrays:
        row_layout.append([(off, size, tuple(b for _, b in halves)) for off, size, halves in segments])
        for _, _, halves in segments:
            operands += [array for array, _ in halves]
    for sources in col_arrays:
        col_layout.append([tuple(b for _, b in source) for source in sources])
        for source in sources:
            operands += [array for array, _ in source]
    in_specs = [pl.BlockSpec(memory_space=pltpu.SMEM)]
    in_specs += [anywhere] * (len(operands) - 1)
    aliases = {}
    scratch = [
        pltpu.VMEM((total, 2 * depth), jnp.bfloat16),
        pltpu.VMEM((width, 2 * depth), jnp.bfloat16),
        pltpu.VMEM((2, tile, held), jnp.int16 if send else jnp.float32),
    ]
    sems = [
        pltpu.SemaphoreType.DMA((len(blocks), max(r.steps for r in blocks), 4, 2)),
        pltpu.SemaphoreType.DMA((len(pieces), 2)),
        pltpu.SemaphoreType.DMA((2, len(pieces))),
    ]
    if send:
        exps = exponent_rows(blocks)
        out_shape = jax.ShapeDtypeStruct((total + exps, width), jnp.int16)
        scratch += [pltpu.VMEM((exps, width), jnp.float32), pltpu.VMEM((exps, width), jnp.int16)]
        sems += [pltpu.SemaphoreType.DMA((1,))]
    else:
        out_shape = jax.ShapeDtypeStruct((2, own_rows, 2 * own_rows), jnp.float32)
        if out is not None:
            operands.append(out)
            in_specs.append(anywhere)
            aliases = {len(operands) - 1: 0}
    return pl.pallas_call(
        functools.partial(mm_kernel, send, active, blocks, pieces, row_layout, col_layout),
        out_shape=(out_shape, jax.ShapeDtypeStruct(TOKEN, jnp.float32)),
        in_specs=in_specs,
        out_specs=(anywhere, pl.BlockSpec(memory_space=pltpu.VMEM)),
        scratch_shapes=scratch + sems,
        input_output_aliases=aliases,
        compiler_params=pltpu.CompilerParams(vmem_limit_bytes=VMEM_LIMIT),
        cost_estimate=pl.CostEstimate(flops=1, bytes_accessed=1, transcendentals=0),
        name="coded_tiles" if send else "result_tiles",
    )(*operands)


def decode_kernel(blocks, pieces, *refs):
    flags, _, *codes, _, out, token, qbuf, ebuf, obuf, qsem, esem, osem = refs
    exps = exponent_rows(blocks)
    cores = len(codes)
    width = sum(n for _, _, n in pieces)
    total = sum(r.mine for r in blocks)
    token[...] = jnp.zeros_like(token)
    work = []
    for core in range(cores):
        row, scale = 0, 0
        for r in blocks:
            for i in range(r.steps):
                work.append((core, r, row, r.lo + core * r.mine + i * r.tile, scale))
                row += r.tile
                scale += r.tile // r.group

    @pl.when(flags[ARRIVE] == 1)
    def _():
        def in_copy(j):
            core, r, row, _, _ = work[j]
            return pltpu.make_async_copy(
                codes[core].at[pl.ds(row, r.tile), :],
                qbuf.at[j, pl.ds(0, r.tile), :],
                qsem.at[j],
            )

        def exp_copy(core):
            return pltpu.make_async_copy(
                codes[core].at[pl.ds(total, exps), :], ebuf.at[core], esem.at[core]
            )

        def out_copy(j):
            _, r, _, lo, _ = work[j]
            return pltpu.make_async_copy(
                obuf.at[j % 2, pl.ds(0, r.tile), :],
                target(flags, out, r, lo, r.tile, *pieces[0][:2], width),
                osem.at[j % 2],
            )

        for core in range(cores):
            exp_copy(core).start()
        for j in range(len(work)):
            in_copy(j).start()
        scales = []
        for core in range(cores):
            exp_copy(core).wait()
            scales.append(jnp.exp2(ebuf[core].astype(jnp.int32).astype(jnp.float32) - 15.0))
        for j, (core, r, _, _, scale) in enumerate(work):
            in_copy(j).wait()
            if j >= 2:
                out_copy(j - 2).wait()
            values = qbuf[j, pl.ds(0, r.tile), :].astype(jnp.int32).astype(jnp.float32)
            for g in range(r.tile // r.group):
                obuf[j % 2, pl.ds(g * r.group, r.group), :] = (
                    values[g * r.group : (g + 1) * r.group] * scales[core][scale + g : scale + g + 1]
                )
            out_copy(j).start()
        for j in range(len(work) - 2, len(work)):
            out_copy(j).wait()


def decode_call(flags, token, coded, out, blocks, pieces):
    width = sum(n for _, _, n in pieces)
    tile = max(r.tile for r in blocks)
    count = len(coded) * sum(r.steps for r in blocks)
    anywhere = pl.BlockSpec(memory_space=pltpu.HBM)
    return pl.pallas_call(
        functools.partial(decode_kernel, blocks, pieces),
        out_shape=(
            jax.ShapeDtypeStruct(out.shape, out.dtype),
            jax.ShapeDtypeStruct(TOKEN, jnp.float32),
        ),
        in_specs=[pl.BlockSpec(memory_space=pltpu.SMEM)] + [anywhere] * (2 + len(coded)),
        out_specs=(anywhere, pl.BlockSpec(memory_space=pltpu.VMEM)),
        scratch_shapes=[
            pltpu.VMEM((count, tile, width), jnp.int16),
            pltpu.VMEM((len(coded), exponent_rows(blocks), width), jnp.int16),
            pltpu.VMEM((2, tile, width), jnp.float32),
            pltpu.SemaphoreType.DMA((count,)),
            pltpu.SemaphoreType.DMA((2,)),
            pltpu.SemaphoreType.DMA((2,)),
        ],
        input_output_aliases={2 + len(coded): 0},
        compiler_params=pltpu.CompilerParams(vmem_limit_bytes=VMEM_LIMIT),
        cost_estimate=pl.CostEstimate(flops=1, bytes_accessed=1, transcendentals=0),
        name="decode_tiles",
    )(flags, token, *coded, out)


def permute(value, move):
    pairs = []
    for r in range(4):
        for c in range(2):
            for s in range(2):
                to = move(r, c, s)
                if to is not None:
                    pairs.append(((r * 2 + c) * 2 + s, (to[0] * 2 + to[1]) * 2 + to[2]))
    return lax.ppermute(value, AXES, pairs)


def inner(r):
    return r in (1, 2)


def far_core(r):
    return 1 - r // 2


def symmetric_shards(chunks, orbital_factors, screen_mask):
    _, own_rows, occupied = orbital_factors.shape
    r, c, s = (lax.axis_index(name) for name in AXES)
    side = r // 2
    t = s ^ side
    inside = jnp.logical_and(r >= 1, r <= 2)
    near = t == 0
    flags = jnp.stack(
        [
            jnp.logical_or(near, inside).astype(jnp.int32),
            inside.astype(jnp.int32),
            jnp.logical_and(jnp.logical_not(near), jnp.logical_not(inside)).astype(jnp.int32),
            t.astype(jnp.int32),
            (jnp.where(near, 1 - r % 2, side) * own_rows).astype(jnp.int32),
            (jnp.where(near, r % 2, 1 - side) * own_rows).astype(jnp.int32),
            c.astype(jnp.int32),
            near.astype(jnp.int32),
            jnp.logical_and(jnp.logical_not(near), inside).astype(jnp.int32),
            jnp.logical_and(near, inside).astype(jnp.int32),
        ]
    )
    per_block = own_rows // BLK
    weights = lax.dynamic_slice(screen_mask, ((c * 4 + r) * per_block, s), (per_block, 1))
    weights = weights.astype(jnp.bfloat16)
    def mask(off, size):
        part = orbital_factors[0, off : off + size].reshape(size // BLK, BLK, occupied)
        part = part * weights[off // BLK : (off + size) // BLK][:, :, None]
        return part.reshape(size, occupied)

    outer_pair = lambda r, c, s: (r ^ 1, c, s)
    mid_pair = lambda r, c, s: (3 - r, c, s) if inner(r) else None
    x_pair = lambda r, c, s: (r, 1 - c, s)
    x_inner = lambda r, c, s: (r, 1 - c, s) if inner(r) else None
    swap = lambda r, c, s: (r, c, 1 - s)
    near_to_far = lambda r, c, s: (r ^ 1, c, 1 - s) if inner(r) and far_core(r) != s else None
    far_to_far = lambda r, c, s: (r ^ 1, c, s) if inner(r) and far_core(r) == s else None

    state = {"out": None, "token": jnp.zeros(TOKEN, jnp.float32)}
    arrays = {}
    moves = {
        "nb": outer_pair, "m1": mid_pair, "m2": mid_pair, "rx": x_pair, "nbx": x_inner,
        "n": near_to_far, "f": far_to_far,
    }
    sources = {"nb": "part", "m1": "part", "rx": "part", "m2": "nb", "nbx": "nb", "n": "code", "f": "code"}

    def tie(value):
        value, state["token"] = lax.optimization_barrier((value, state["token"]))
        return value

    def start(kind, k):
        arrays[kind, k] = permute(tie(arrays[sources[kind], k]), moves[kind])

    def done(kind, k):
        arrays[kind, k] = tie(arrays[kind, k])

    def start_swap(kind, k):
        arrays[kind + "_h", k] = permute(tie(arrays[kind, k]), swap)

    def done_swap(kind, k):
        arrays[kind + "_h", k] = tie(arrays[kind + "_h", k])


    def halves(kind, k):
        return (arrays[kind, k], 0), (arrays[kind + "_h", k], 0)

    def rows_of(kinds, cores):
        blocks, segments = [], []
        for kind, which in kinds:
            lo = chunks[which[0]][0]
            count = sum(chunks[k][1] for k in which)
            blocks.append(Rows(int(kind in ("nbx", "rx")), lo, count, cores))
            segments.append([(*chunks[k], halves(kind, k)) for k in which])
        return blocks, segments

    def pieces_of(where):
        return [(second, *chunks[k]) for second, k in where]

    def coded(name, kinds, *where, cores=2):
        blocks, rows = rows_of(kinds, cores)
        cols = [[halves(("m1", "m2")[second], k)] for second, k in where]
        arrays["code", name], state["token"] = mm_call(
            flags, state["token"], True, CODED if cores == 2 else CODED_NEAR, blocks, rows,
            pieces_of(where), cols, None, own_rows,
        )
        arrays["item", name] = (blocks, pieces_of(where))

    def result(kinds, *where, active=RESULT):
        blocks, rows = rows_of(kinds, 1)
        names = (("nb", "m1"), {RESULT: ("own", "m2"), NEAR: ("own",), FAR_INSIDE: ("m2",)}[active])
        cols = [[halves(kind, k) for kind in names[second]] for second, k in where]
        state["out"], state["token"] = mm_call(
            flags, state["token"], False, active, blocks, rows, pieces_of(where), cols, state["out"],
            own_rows,
        )

    def decode(name):
        state["out"], state["token"] = decode_call(
            flags, state["token"], [arrays[kind, name] for kind in "nf" if (kind, name) in arrays],
            state["out"], *arrays["item", name],
        )

    for k, chunk in enumerate(chunks):
        arrays["part", k] = arrays["own", k] = mask(*chunk)
    both = [0, 1]

    start("nb", 0)
    start("m1", 0)
    start("rx", 0)
    start_swap("own", 0)
    start_swap("own", 1)
    done_swap("own", 0)
    done_swap("own", 1)
    done("nb", 0)
    done("m1", 0)
    done("rx", 0)
    start("nb", 1)
    start("m1", 1)
    start("nbx", 0)
    start_swap("nb", 0)
    start_swap("m1", 0)
    start_swap("rx", 0)
    done_swap("nb", 0)
    done_swap("m1", 0)
    done_swap("rx", 0)
    result([("own", both), ("rx", [0])], (0, 0))
    result([("own", both)], (1, 0), (1, 1), active=NEAR)
    done("nb", 1)
    done("m1", 1)
    done("nbx", 0)
    start("m2", 1)
    start("nbx", 1)
    start_swap("nb", 1)
    start_swap("m1", 1)
    start_swap("nbx", 0)
    done_swap("nb", 1)
    done_swap("m1", 1)
    done_swap("nbx", 0)
    coded(0, [("nb", both)], (0, 0), (0, 1))
    start("n", 0)
    start("f", 0)
    coded(1, [("nbx", [0])], (0, 0), (0, 1))
    result([("own", both), ("rx", [0])], (0, 1))
    done("m2", 1)
    done("nbx", 1)
    done("n", 0)
    done("f", 0)
    start("m2", 0)
    start("n", 1)
    start("f", 1)
    start_swap("m2", 1)
    start_swap("nbx", 1)
    done_swap("m2", 1)
    done_swap("nbx", 1)
    start("rx", 1)
    coded(2, [("nbx", [1])], (0, 0), (0, 1))
    done("n", 1)
    done("f", 1)
    start("n", 2)
    start("f", 2)
    coded(3, [("nb", both), ("nbx", both)], (1, 1))
    done("m2", 0)
    done("n", 2)
    done("f", 2)
    start("n", 3)
    start("f", 3)
    start_swap("m2", 0)
    done_swap("m2", 0)
    coded(4, [("nb", both), ("nbx", both)], (1, 0), cores=1)
    result([("rx", [0])], (1, 0), (1, 1), active=NEAR)
    result([("own", both), ("rx", [0])], (1, 1), active=FAR_INSIDE)
    result([("own", both), ("rx", [0])], (1, 0), active=FAR_INSIDE)
    done("n", 3)
    done("f", 3)
    start("n", 4)
    done("rx", 1)
    start_swap("rx", 1)
    for name in range(4):
        decode(name)
    done_swap("rx", 1)
    result([("rx", [1])], (0, 0), (0, 1), (1, 1), (1, 0))
    decode(4)
    return state["out"]


def split_rows(own_rows):
    size = own_rows // BLK // 2 * BLK
    return [(0, size), (size, own_rows - size)]


def solution(mesh):
    placed = (P("sub", ("groups", "col", "row"), None), P("groups", None))
    result = P(None, ("groups", "row"), ("col", "sub"))

    def shards(orbital_factors, screen_mask):
        aux_half, own_rows, _ = orbital_factors.shape
        small = (mesh.shape["row"], mesh.shape["col"], mesh.shape["sub"]) == (4, 2, 2)
        if small and aux_half == 1 and own_rows == 11 * BLK:
            return symmetric_shards(split_rows(own_rows), orbital_factors, screen_mask)
        return gathered_shards(orbital_factors, screen_mask)

    return jax.shard_map(
        shards, mesh=mesh, in_specs=placed, out_specs=result, check_vma=False
    )
```

```python
import functools

import jax
import jax.numpy as jnp
from jax import lax
from jax.experimental import pallas as pl
from jax.experimental.pallas import tpu as pltpu
from jax.sharding import PartitionSpec as P

BLK = 128
AXES = ("row", "col", "sub")
MAX_GROUP = 88
VMEM_LIMIT = 63 * 2**20
TOKEN = (8, 128)


def apply_screen(panel, first_row, screen_mask, aux_start):
    row_total = panel.shape[1]
    block_ids = (first_row + jnp.arange(row_total, dtype=jnp.int32)) // BLK
    one_hot = (
        block_ids[:, None] == jnp.arange(screen_mask.shape[0], dtype=jnp.int32)[None, :]
    ).astype(jnp.float32)
    row_weights = jnp.dot(
        one_hot, screen_mask.astype(jnp.float32), preferred_element_type=jnp.float32
    )
    row_weights = lax.dynamic_slice_in_dim(row_weights, aux_start, panel.shape[0], 1)
    return panel * jnp.transpose(row_weights).astype(jnp.bfloat16)[:, :, None]


def gathered_shards(orbital_factors, screen_mask):
    aux_half, own_rows, occupied = orbital_factors.shape
    row_count = lax.axis_size("row")
    col_count = lax.axis_size("col")
    row_pos = lax.axis_index("row")
    col_pos = lax.axis_index("col")
    sub_pos = lax.axis_index("sub")
    own_first = (col_pos * row_count + row_pos) * own_rows
    screened = apply_screen(orbital_factors, own_first, screen_mask, sub_pos * aux_half)
    contract_dims = (((0, 2), (0, 2)), ((), ()))
    gathered_rows = lax.all_gather(screened, "col", axis=1, tiled=True)
    partial_tile = lax.dot_general(
        gathered_rows,
        lax.all_gather(screened, "row", axis=1, tiled=True),
        contract_dims,
        preferred_element_type=jnp.float32,
    )
    tile_sum = lax.psum_scatter(partial_tile, "sub", scatter_dimension=1, tiled=True)
    return tile_sum.reshape(col_count, own_rows, tile_sum.shape[1])


RESULT, CODED, ARRIVE, FAR, BASE1, BASE2, COLUMN, NEAR, FAR_INSIDE, CODED_NEAR = range(10)


def encode(acc, group):
    coded, exps = [], []
    for first in range(0, acc.shape[0], group):
        part = acc[first : first + group]
        top = jnp.max(jnp.abs(part), axis=0, keepdims=True)
        exp = jnp.floor(jnp.log2(jnp.maximum(top, 2.0**-100))) + 1.0
        scaled = jnp.round(part * jnp.exp2(15.0 - exp))
        coded.append(jnp.clip(scaled, -32767.0, 32767.0).astype(jnp.int32))
        exps.append(exp)
    return jnp.concatenate(coded, axis=0).astype(jnp.int16), exps


class Rows:
    def __init__(self, block, lo, count, cores):
        self.block, self.lo, self.count = block, lo, count
        self.mine = count // cores
        self.steps = 2 if self.mine < 1024 else 4
        self.tile = self.mine // self.steps
        self.group = max(g for g in range(8, MAX_GROUP + 1, 8) if self.tile % g == 0)


def exponent_rows(blocks):
    return -(-sum(r.mine // r.group for r in blocks) // 16) * 16


def overlap(segments, lo, hi):
    parts = []
    for k, (off, size) in enumerate(segments):
        first, last = max(lo, off), min(hi, off + size)
        if first < last:
            parts.append((k, first - off, last - first, first - lo))
    return parts


def target(flags, out, rows, lo, count, second, col, width):
    a = flags[COLUMN] if rows.block == 0 else 1 - flags[COLUMN]
    base = pl.multiple_of(flags[BASE2 if second else BASE1] + col, 128)
    return out.at[a, pl.ds(lo, count), pl.ds(base, width)]


def groups_of(blocks, pieces):
    if len(blocks) == 1:
        return [(0, [p]) for p in range(len(pieces))]
    return [(b, list(range(len(pieces)))) for b in range(len(blocks))]


def locals_of(pieces):
    return [sum(n for _, _, n in pieces[:p]) for p in range(len(pieces))]


def mm_kernel(send, active, blocks, pieces, row_layout, col_layout, *refs):
    it = iter(refs)
    flags = next(it)
    next(it)
    rows = [[[next(it) for _ in range(2)] for _ in segments] for segments in row_layout]
    cols = [[[next(it) for _ in range(2)] for _ in sources] for sources in col_layout]
    rest = list(it)
    if send:
        out, token, rowbuf, colbuf, obuf, ebuf, ecode, rsem, csem, osem, esem = rest
    else:
        out, token, rowbuf, colbuf, obuf, rsem, csem, osem = rest[-8:]
    depth = rows[0][0][0].shape[1]
    begins = locals_of(pieces)
    firsts = [sum(r.mine for r in blocks[:b]) for b in range(len(blocks))]
    total = sum(r.mine for r in blocks)
    groups = groups_of(blocks, pieces)
    token[...] = jnp.zeros_like(token)

    def col_copy(p, aux, core):
        size = pieces[p][2]
        return pltpu.make_async_copy(
            cols[p][core][aux].at[pl.ds(col_layout[p][core][aux], size), :],
            colbuf.at[pl.ds(begins[p], size), pl.ds(aux * depth, depth)],
            csem.at[p, aux],
        )

    def row_copies(b, i, core):
        r = blocks[b]
        lo = r.lo + core * r.mine + i * r.tile
        spans = [(off, size) for off, size, _ in row_layout[b]]
        made = []
        for j, (k, off, size, local) in enumerate(overlap(spans, lo, lo + r.tile)):
            for aux in range(2):
                made.append(
                    pltpu.make_async_copy(
                        rows[b][k][aux].at[pl.ds(row_layout[b][k][2][aux] + off, size), :],
                        rowbuf.at[
                            pl.ds(firsts[b] + i * r.tile + local, size), pl.ds(aux * depth, depth)
                        ],
                        rsem.at[b, i, j, aux],
                    )
                )
        return made

    def per_core(act):
        for core in range(2):

            @pl.when(flags[FAR] == core)
            def _():
                act(core)

    def out_copies(g, i, slot):
        b, members = groups[g]
        r = blocks[b]
        if send:
            held = sum(pieces[p][2] for p in members)
            where = out.at[pl.ds(firsts[b] + i * r.tile, r.tile), pl.ds(begins[members[0]], held)]
            source = obuf.at[slot, pl.ds(0, r.tile), pl.ds(0, held)]
            return [pltpu.make_async_copy(source, where, osem.at[slot, 0])]
        made = []
        for p in members:
            second, off, n = pieces[p]
            where = target(flags, out, r, r.lo + i * r.tile, r.tile, second, off, n)
            source = obuf.at[slot, pl.ds(0, r.tile), pl.ds(begins[p] - begins[members[0]], n)]
            made.append(pltpu.make_async_copy(source, where, osem.at[slot, p]))
        return made

    def out_start(g, i, slot):
        for copy in out_copies(g, i, slot):
            copy.start()

    def out_wait(g, i, slot):
        for copy in out_copies(g, i, slot):
            copy.wait()

    def exp_copy():
        return pltpu.make_async_copy(
            ecode, out.at[pl.ds(total, exponent_rows(blocks)), :], esem.at[0]
        )

    @pl.when(flags[active] == 1)
    def _():
        def load(j):
            def begin(core):
                for aux in range(2):
                    col_copy(j, aux, core if len(cols[j]) > 1 else 0).start()

            if len(cols[j]) > 1:
                per_core(begin)
            else:
                begin(0)

        def load_rows(b, step):
            def begin(core):
                for copy in row_copies(b, step, core):
                    copy.start()

            if send:
                per_core(begin)
            else:
                begin(0)

        def wait_rows(b, step):
            def arrive(core):
                for copy in row_copies(b, step, core):
                    copy.wait()

            if send:
                per_core(arrive)
            else:
                arrive(0)

        def load_next(b, step):
            if step + 1 < blocks[b].steps:
                load_rows(b, step + 1)
            elif b + 1 < len(blocks):
                load_rows(b + 1, 0)

        def multiply(b, i, slot, local, size, place, scales):
            r = blocks[b]
            acc = lax.dot_general(
                rowbuf[pl.ds(pl.multiple_of(firsts[b] + i * r.tile, 16), r.tile), :],
                colbuf[pl.ds(local, size), :],
                (((1,), (1,)), ((), ())),
                preferred_element_type=jnp.float32,
            )
            if send:
                acc, exps = encode(acc, r.group)
                for g, exp in enumerate(exps):
                    pos = scales + i * (r.tile // r.group) + g
                    ebuf[pl.ds(pos, 1), pl.ds(local, size)] = exp
            obuf[slot, pl.ds(0, r.tile), pl.ds(place, size)] = acc

        load(0)
        load_rows(0, 0)
        for p in range(1, len(groups[0][1])):
            load(p)
        if send:
            ebuf[...] = jnp.zeros_like(ebuf)
        for g, (b, members) in enumerate(groups):
            r = blocks[b]
            scales = sum(other.mine // other.group for other in blocks[:b])
            new_rows = g == 0 or groups[g - 1][0] != b
            new_cols = [p for p in members if all(p not in group[1] for group in groups[:g])]

            def body(i, carry, g=g, b=b, r=r, members=members, new_rows=new_rows, new_cols=new_cols, scales=scales):
                if new_rows:
                    for step in range(r.steps):

                        @pl.when(i == step)
                        def _(step=step):
                            wait_rows(b, step)
                            load_next(b, step)

                slot = lax.rem(i, 2)

                @pl.when(i >= 2)
                def _():
                    out_wait(g, i - 2, slot)

                if g > 0:

                    @pl.when(i < 2)
                    def _():
                        out_wait(g - 1, blocks[groups[g - 1][0]].steps - 2 + i, slot)

                for p in members:
                    if p in new_cols:

                        @pl.when(i == 0)
                        def _(p=p):
                            for aux in range(2):
                                col_copy(p, aux, 0).wait()
                            if g + 1 < len(groups) and p == new_cols[-1]:
                                for later in groups[g + 1][1]:
                                    if later not in members:
                                        load(later)

                    multiply(b, i, slot, begins[p], pieces[p][2], begins[p] - begins[members[0]], scales)
                out_start(g, i, slot)
                return carry

            lax.fori_loop(0, r.steps, body, 0)
        if send:
            ecode[...] = ebuf[...].astype(jnp.int32).astype(jnp.int16)
            exp_copy().start()
        for slot in range(2):
            out_wait(len(groups) - 1, blocks[-1].steps - 2 + slot, slot)
        if send:
            exp_copy().wait()


def mm_call(flags, token, send, active, blocks, row_arrays, pieces, col_arrays, out, own_rows):
    width = sum(n for _, _, n in pieces)
    depth = row_arrays[0][0][2][0][0].shape[1]
    total = sum(r.mine for r in blocks)
    tile = max(r.tile for r in blocks)
    held = max(sum(pieces[p][2] for p in ps) for _, ps in groups_of(blocks, pieces))
    anywhere = pl.BlockSpec(memory_space=pltpu.HBM)
    operands = [flags, token]
    row_layout, col_layout = [], []
    for segments in row_arrays:
        row_layout.append([(off, size, tuple(b for _, b in halves)) for off, size, halves in segments])
        for _, _, halves in segments:
            operands += [array for array, _ in halves]
    for sources in col_arrays:
        col_layout.append([tuple(b for _, b in source) for source in sources])
        for source in sources:
            operands += [array for array, _ in source]
    in_specs = [pl.BlockSpec(memory_space=pltpu.SMEM)]
    in_specs += [anywhere] * (len(operands) - 1)
    aliases = {}
    scratch = [
        pltpu.VMEM((total, 2 * depth), jnp.bfloat16),
        pltpu.VMEM((width, 2 * depth), jnp.bfloat16),
        pltpu.VMEM((2, tile, held), jnp.int16 if send else jnp.float32),
    ]
    sems = [
        pltpu.SemaphoreType.DMA((len(blocks), max(r.steps for r in blocks), 4, 2)),
        pltpu.SemaphoreType.DMA((len(pieces), 2)),
        pltpu.SemaphoreType.DMA((2, len(pieces))),
    ]
    if send:
        exps = exponent_rows(blocks)
        out_shape = jax.ShapeDtypeStruct((total + exps, width), jnp.int16)
        scratch += [pltpu.VMEM((exps, width), jnp.float32), pltpu.VMEM((exps, width), jnp.int16)]
        sems += [pltpu.SemaphoreType.DMA((1,))]
    else:
        out_shape = jax.ShapeDtypeStruct((2, own_rows, 2 * own_rows), jnp.float32)
        if out is not None:
            operands.append(out)
            in_specs.append(anywhere)
            aliases = {len(operands) - 1: 0}
    return pl.pallas_call(
        functools.partial(mm_kernel, send, active, blocks, pieces, row_layout, col_layout),
        out_shape=(out_shape, jax.ShapeDtypeStruct(TOKEN, jnp.float32)),
        in_specs=in_specs,
        out_specs=(anywhere, pl.BlockSpec(memory_space=pltpu.VMEM)),
        scratch_shapes=scratch + sems,
        input_output_aliases=aliases,
        compiler_params=pltpu.CompilerParams(vmem_limit_bytes=VMEM_LIMIT),
        cost_estimate=pl.CostEstimate(flops=1, bytes_accessed=1, transcendentals=0),
        name="coded_tiles" if send else "result_tiles",
    )(*operands)


def decode_kernel(blocks, pieces, *refs):
    flags, _, *codes, _, out, token, qbuf, ebuf, obuf, qsem, esem, osem = refs
    exps = exponent_rows(blocks)
    cores = len(codes)
    width = sum(n for _, _, n in pieces)
    total = sum(r.mine for r in blocks)
    token[...] = jnp.zeros_like(token)
    work = []
    for core in range(cores):
        row, scale = 0, 0
        for r in blocks:
            for i in range(r.steps):
                work.append((core, r, row, r.lo + core * r.mine + i * r.tile, scale))
                row += r.tile
                scale += r.tile // r.group

    @pl.when(flags[ARRIVE] == 1)
    def _():
        def in_copy(j):
            core, r, row, _, _ = work[j]
            return pltpu.make_async_copy(
                codes[core].at[pl.ds(row, r.tile), :],
                qbuf.at[j, pl.ds(0, r.tile), :],
                qsem.at[j],
            )

        def exp_copy(core):
            return pltpu.make_async_copy(
                codes[core].at[pl.ds(total, exps), :], ebuf.at[core], esem.at[core]
            )

        def out_copy(j):
            _, r, _, lo, _ = work[j]
            return pltpu.make_async_copy(
                obuf.at[j % 2, pl.ds(0, r.tile), :],
                target(flags, out, r, lo, r.tile, *pieces[0][:2], width),
                osem.at[j % 2],
            )

        for core in range(cores):
            exp_copy(core).start()
        for j in range(len(work)):
            in_copy(j).start()
        scales = []
        for core in range(cores):
            exp_copy(core).wait()
            scales.append(jnp.exp2(ebuf[core].astype(jnp.int32).astype(jnp.float32) - 15.0))
        for j, (core, r, _, _, scale) in enumerate(work):
            in_copy(j).wait()
            if j >= 2:
                out_copy(j - 2).wait()
            values = qbuf[j, pl.ds(0, r.tile), :].astype(jnp.int32).astype(jnp.float32)
            for g in range(r.tile // r.group):
                obuf[j % 2, pl.ds(g * r.group, r.group), :] = (
                    values[g * r.group : (g + 1) * r.group] * scales[core][scale + g : scale + g + 1]
                )
            out_copy(j).start()
        for j in range(len(work) - 2, len(work)):
            out_copy(j).wait()


def decode_call(flags, token, coded, out, blocks, pieces):
    width = sum(n for _, _, n in pieces)
    tile = max(r.tile for r in blocks)
    count = len(coded) * sum(r.steps for r in blocks)
    anywhere = pl.BlockSpec(memory_space=pltpu.HBM)
    return pl.pallas_call(
        functools.partial(decode_kernel, blocks, pieces),
        out_shape=(
            jax.ShapeDtypeStruct(out.shape, out.dtype),
            jax.ShapeDtypeStruct(TOKEN, jnp.float32),
        ),
        in_specs=[pl.BlockSpec(memory_space=pltpu.SMEM)] + [anywhere] * (2 + len(coded)),
        out_specs=(anywhere, pl.BlockSpec(memory_space=pltpu.VMEM)),
        scratch_shapes=[
            pltpu.VMEM((count, tile, width), jnp.int16),
            pltpu.VMEM((len(coded), exponent_rows(blocks), width), jnp.int16),
            pltpu.VMEM((2, tile, width), jnp.float32),
            pltpu.SemaphoreType.DMA((count,)),
            pltpu.SemaphoreType.DMA((2,)),
            pltpu.SemaphoreType.DMA((2,)),
        ],
        input_output_aliases={2 + len(coded): 0},
        compiler_params=pltpu.CompilerParams(vmem_limit_bytes=VMEM_LIMIT),
        cost_estimate=pl.CostEstimate(flops=1, bytes_accessed=1, transcendentals=0),
        name="decode_tiles",
    )(flags, token, *coded, out)


def permute(value, move):
    pairs = []
    for r in range(4):
        for c in range(2):
            for s in range(2):
                to = move(r, c, s)
                if to is not None:
                    pairs.append(((r * 2 + c) * 2 + s, (to[0] * 2 + to[1]) * 2 + to[2]))
    return lax.ppermute(value, AXES, pairs)


def inner(r):
    return r in (1, 2)


def far_core(r):
    return 1 - r // 2


def symmetric_shards(chunks, orbital_factors, screen_mask):
    _, own_rows, occupied = orbital_factors.shape
    r, c, s = (lax.axis_index(name) for name in AXES)
    side = r // 2
    t = s ^ side
    inside = jnp.logical_and(r >= 1, r <= 2)
    near = t == 0
    flags = jnp.stack(
        [
            jnp.logical_or(near, inside).astype(jnp.int32),
            inside.astype(jnp.int32),
            jnp.logical_and(jnp.logical_not(near), jnp.logical_not(inside)).astype(jnp.int32),
            t.astype(jnp.int32),
            (jnp.where(near, 1 - r % 2, side) * own_rows).astype(jnp.int32),
            (jnp.where(near, r % 2, 1 - side) * own_rows).astype(jnp.int32),
            c.astype(jnp.int32),
            near.astype(jnp.int32),
            jnp.logical_and(jnp.logical_not(near), inside).astype(jnp.int32),
            jnp.logical_and(near, inside).astype(jnp.int32),
        ]
    )
    per_block = own_rows // BLK
    weights = lax.dynamic_slice(screen_mask, ((c * 4 + r) * per_block, s), (per_block, 1))
    weights = weights.astype(jnp.bfloat16)
    def mask(off, size):
        part = orbital_factors[0, off : off + size].reshape(size // BLK, BLK, occupied)
        part = part * weights[off // BLK : (off + size) // BLK][:, :, None]
        return part.reshape(size, occupied)

    outer_pair = lambda r, c, s: (r ^ 1, c, s)
    mid_pair = lambda r, c, s: (3 - r, c, s) if inner(r) else None
    x_pair = lambda r, c, s: (r, 1 - c, s)
    x_inner = lambda r, c, s: (r, 1 - c, s) if inner(r) else None
    swap = lambda r, c, s: (r, c, 1 - s)
    near_to_far = lambda r, c, s: (r ^ 1, c, 1 - s) if inner(r) and far_core(r) != s else None
    far_to_far = lambda r, c, s: (r ^ 1, c, s) if inner(r) and far_core(r) == s else None

    state = {"out": None, "token": jnp.zeros(TOKEN, jnp.float32)}
    arrays = {}
    moves = {
        "nb": outer_pair, "m1": mid_pair, "m2": mid_pair, "rx": x_pair, "nbx": x_inner,
        "n": near_to_far, "f": far_to_far,
    }
    sources = {"nb": "part", "m1": "part", "rx": "part", "m2": "nb", "nbx": "nb", "n": "code", "f": "code"}

    def tie(value):
        value, state["token"] = lax.optimization_barrier((value, state["token"]))
        return value

    def start(kind, k):
        arrays[kind, k] = permute(tie(arrays[sources[kind], k]), moves[kind])

    def done(kind, k):
        arrays[kind, k] = tie(arrays[kind, k])

    def start_swap(kind, k):
        arrays[kind + "_h", k] = permute(tie(arrays[kind, k]), swap)

    def done_swap(kind, k):
        arrays[kind + "_h", k] = tie(arrays[kind + "_h", k])


    def halves(kind, k):
        return (arrays[kind, k], 0), (arrays[kind + "_h", k], 0)

    def rows_of(kinds, cores):
        blocks, segments = [], []
        for kind, which in kinds:
            lo = chunks[which[0]][0]
            count = sum(chunks[k][1] for k in which)
            blocks.append(Rows(int(kind in ("nbx", "rx")), lo, count, cores))
            segments.append([(*chunks[k], halves(kind, k)) for k in which])
        return blocks, segments

    def pieces_of(where):
        return [(second, *chunks[k]) for second, k in where]

    def coded(name, kinds, *where, cores=2):
        blocks, rows = rows_of(kinds, cores)
        cols = [[halves(("m1", "m2")[second], k)] for second, k in where]
        arrays["code", name], state["token"] = mm_call(
            flags, state["token"], True, CODED if cores == 2 else CODED_NEAR, blocks, rows,
            pieces_of(where), cols, None, own_rows,
        )
        arrays["item", name] = (blocks, pieces_of(where))

    def result(kinds, *where, active=RESULT):
        blocks, rows = rows_of(kinds, 1)
        names = (("nb", "m1"), {RESULT: ("own", "m2"), NEAR: ("own",), FAR_INSIDE: ("m2",)}[active])
        cols = [[halves(kind, k) for kind in names[second]] for second, k in where]
        state["out"], state["token"] = mm_call(
            flags, state["token"], False, active, blocks, rows, pieces_of(where), cols, state["out"],
            own_rows,
        )

    def decode(name):
        state["out"], state["token"] = decode_call(
            flags, state["token"], [arrays[kind, name] for kind in "nf" if (kind, name) in arrays],
            state["out"], *arrays["item", name],
        )

    for k, chunk in enumerate(chunks):
        arrays["part", k] = arrays["own", k] = mask(*chunk)
    both = [0, 1]

    start("nb", 0)
    start("m1", 0)
    start("rx", 0)
    start_swap("own", 0)
    start_swap("own", 1)
    done_swap("own", 0)
    done_swap("own", 1)
    done("nb", 0)
    done("m1", 0)
    done("rx", 0)
    start("nb", 1)
    start("m1", 1)
    start("nbx", 0)
    start_swap("nb", 0)
    start_swap("m1", 0)
    start_swap("rx", 0)
    done_swap("nb", 0)
    done_swap("m1", 0)
    done_swap("rx", 0)
    result([("own", both), ("rx", [0])], (0, 0))
    result([("own", both)], (1, 0), (1, 1), active=NEAR)
    done("nb", 1)
    done("m1", 1)
    done("nbx", 0)
    start("m2", 1)
    start("nbx", 1)
    start_swap("nb", 1)
    start_swap("m1", 1)
    start_swap("nbx", 0)
    done_swap("nb", 1)
    done_swap("m1", 1)
    done_swap("nbx", 0)
    coded(0, [("nb", both)], (0, 0), (0, 1))
    start("n", 0)
    start("f", 0)
    coded(1, [("nbx", [0])], (0, 0), (0, 1))
    result([("own", both), ("rx", [0])], (0, 1))
    done("m2", 1)
    done("nbx", 1)
    done("n", 0)
    done("f", 0)
    start("m2", 0)
    start("n", 1)
    start("f", 1)
    start_swap("m2", 1)
    start_swap("nbx", 1)
    done_swap("m2", 1)
    done_swap("nbx", 1)
    start("rx", 1)
    coded(2, [("nbx", [1])], (0, 0), (0, 1))
    done("n", 1)
    done("f", 1)
    start("n", 2)
    start("f", 2)
    coded(3, [("nb", both), ("nbx", both)], (1, 1))
    done("m2", 0)
    done("n", 2)
    done("f", 2)
    start("n", 3)
    start("f", 3)
    start_swap("m2", 0)
    done_swap("m2", 0)
    coded(4, [("nb", both), ("nbx", both)], (1, 0), cores=1)
    result([("rx", [0])], (1, 0), (1, 1), active=NEAR)
    result([("own", both), ("rx", [0])], (1, 1), active=FAR_INSIDE)
    result([("own", both), ("rx", [0])], (1, 0), active=FAR_INSIDE)
    done("n", 3)
    done("f", 3)
    start("n", 4)
    done("rx", 1)
    start_swap("rx", 1)
    for name in range(4):
        decode(name)
    done_swap("rx", 1)
    result([("rx", [1])], (0, 0), (0, 1), (1, 1), (1, 0))
    decode(4)
    return state["out"]


def split_rows(own_rows):
    size = own_rows // BLK // 2 * BLK
    return [(0, size), (size, own_rows - size)]


def solution(mesh):
    placed = (P("sub", ("groups", "col", "row"), None), P("groups", None))
    result = P(None, ("groups", "row"), ("col", "sub"))

    def shards(orbital_factors, screen_mask):
        aux_half, own_rows, _ = orbital_factors.shape
        small = (mesh.shape["row"], mesh.shape["col"], mesh.shape["sub"]) == (4, 2, 2)
        if small and aux_half == 1 and own_rows == 11 * BLK:
            return symmetric_shards(split_rows(own_rows), orbital_factors, screen_mask)
        return gathered_shards(orbital_factors, screen_mask)

    return jax.shard_map(
        shards, mesh=mesh, in_specs=placed, out_specs=result, check_vma=False
    )
```
